256 devices in a mesh: mass: 64 (over z, y, core), spec: 4 (over x).
Axes of the slice: x: 4, y: 4, z: 8, core: 2. Of those that a mesh axis runs over, the one named last changes fastest.
Arguments:
- spectra: bfloat16 [8192, 16, 2048], P(('mass', 'spec')), may hold values from -64 to 64
- block_start: int32 [8192], P(('mass', 'spec')), may hold values from 0 to 62, as said below
- block_range: int32 [8192, 2], P(('mass', 'spec')), may hold values from 0 to 4095, as said below
- block_count: int32 [8192], P(('mass', 'spec')), may hold values from 1 to 16
- peptide_table: bfloat16 [65536, 2048], P('mass'), may hold values from -1 to 1
- peptide_bin: int32 [65536], P('mass'), may hold values from 0 to 4095, as said below
- peptide_shift: float32 [65536], P('mass'), may hold values from -4 to 4
Outputs:
- spectrum_lse: float32 [8192, 16], P(('mass', 'spec'))
- spectrum_shift: float32 [8192, 16], P(('mass', 'spec'))
- peptide_support: float32 [65536], P(('mass', 'spec'))
The draws below stay inside these ranges and needn't reach their ends.
Inputs may be any that keep to these rules, and one draw needn't show every extreme that they name: Block b is routed to mass ranges block_start[b] to block_start[b] + 1. No two blocks of one device have the same start, so at most 2 blocks of one device cover one mass range. block_start[b] * 64 <= block_range[b, 0] < block_start[b] * 64 + 64 // 2, block_range[b, 0] + 32 <= block_range[b, 1] < (block_start[b] + 2) * 64. `peptide_bin`: peptides of mass range o have bins from o * 64 to (o + 1) * 64 - 1, and every one of these 64 bins holds at least one peptide.
All inputs are finite; a program needn't handle non-finite values.
Results may differ from the reference program's by a relative error of at most 0.0021.
Values may be sent and summed in bfloat16 or wider, within the bound.
No kernel may reach another device: no remote copies, remote signals or barrier semaphores. Data moves between devices by JAX's collectives and lax.ppermute only.
A program may use at most 64 MiB of HBM per device.

```python
import math
import jax
import jax.numpy as jnp
from jax import lax

B = 2048
PEP_DEV = 1024
SB = 16
WIN = 2
BIN_DEV = 64
BLK_DEV = 32
NBLOCKS = 8192
PEPTIDES = 65536
N_MASS = 64
N_SPEC = 4


def start_table(key):
    key = jax.random.fold_in(key, 101)
    hot_key, order_key = jax.random.split(key)
    hot = jax.random.randint(hot_key, (), 0, N_MASS - 2 * WIN + 2)
    others = N_MASS - 2 * WIN + 1

    def one_device(device_key):
        first_key, second_key = jax.random.split(device_key)
        rest = jax.random.permutation(first_key, others)[:BLK_DEV - WIN]
        rest = rest + WIN * (rest >= hot).astype(rest.dtype)
        hot_run = hot + jnp.arange(WIN)
        joined = jnp.concatenate([hot_run, rest]).astype(jnp.int32)
        return jax.random.permutation(second_key, joined)
    device_keys = jax.random.split(order_key, N_MASS * N_SPEC)
    return jax.vmap(one_device)(device_keys).reshape(-1).astype(jnp.int32)


def range_table(key, starts):
    key = jax.random.fold_in(key, 202)
    low_key, span_key = jax.random.split(key)
    lower = starts * BIN_DEV + jax.random.randint(low_key, starts.shape, 0, BIN_DEV // 2)
    upper = lower + jax.random.randint(span_key, starts.shape, BIN_DEV // 2, (WIN - 1) * BIN_DEV + 1)
    return jnp.stack([lower, upper], axis=1).astype(jnp.int32)


def peptide_rows(key, rows):
    base = jax.random.fold_in(key, 303)

    def one_row(index):
        return jax.random.truncated_normal(jax.random.fold_in(base, index), -4.0, 4.0, (B,), jnp.float32)
    return jax.vmap(one_row)(rows)


def draw_block_start(key, part):
    return start_table(key)


def draw_block_range(key, part):
    return range_table(key, start_table(key))


def draw_peptide_bin(key, part):
    key = jax.random.fold_in(key, 11)
    group = PEP_DEV // BIN_DEV
    local = jnp.arange(PEP_DEV, dtype=jnp.int32) // group
    jitter = jax.random.randint(key, (N_MASS, PEP_DEV), 0, 2)
    bins = jnp.minimum(local[None, :] + jitter, BIN_DEV - 1) + jnp.arange(N_MASS, dtype=jnp.int32)[:, None] * BIN_DEV
    return bins.reshape(-1).astype(jnp.int32)


def draw_peptide_table(key, part):
    rows = peptide_rows(key, jnp.arange(N_MASS * PEP_DEV))
    return (rows / math.sqrt(B)).astype(jnp.bfloat16)


def draw_spectra(key, part):
    own_key = jax.random.fold_in(key, 31)
    value_key, row_key, col_key = jax.random.split(own_key, 3)
    shape = (NBLOCKS, SB, B)
    row_scale = jnp.exp(jax.random.uniform(row_key, (NBLOCKS, SB, 1), jnp.float32, math.log(1.5), math.log(8.0)))
    col_scale = jnp.exp(jax.random.uniform(col_key, (1, 1, B), jnp.float32, math.log(0.5), math.log(2.0)))
    values = jax.random.truncated_normal(value_key, -4.0, 4.0, shape, jnp.float32) * row_scale * col_scale
    return values.astype(jnp.bfloat16)


def touch_ends(values, key, least, high):
    longest = values.shape.index(max(values.shape))
    spots = []
    for shift in (0, 1):
        where = [jax.random.randint(jax.random.fold_in(key, axis), (), 0, length) for axis, length in enumerate(values.shape)]
        where[longest] = (where[longest] + shift) % values.shape[longest]
        spots.append(tuple(where))
    return values.at[spots[0]].set(least).at[spots[1]].set(high)


def block_levels(stream_key, extent, shards, least, high):
    def one(axis_at, blocks):
        heights = jax.random.uniform(jax.random.fold_in(jax.random.fold_in(stream_key, 6), axis_at), (blocks,), jnp.float32, least / len(shards), high / len(shards))
        return jnp.repeat(jnp.exp(heights), extent[axis_at] // blocks).reshape((-1,) + (1,) * (len(extent) - axis_at - 1))

    level = one(*shards[0])
    for cut in shards[1:]:
        level = level * one(*cut)
    return level


def setup_inputs(seed: int = 0) -> dict:
    streams_of = jax.random.split(jax.random.key(seed), 8)
    spectra = draw_spectra(jax.random.fold_in(streams_of[7], 71), 0)
    block_start = draw_block_start(jax.random.fold_in(streams_of[7], 71), 0)
    block_range = draw_block_range(jax.random.fold_in(streams_of[7], 71), 0)
    block_count = touch_ends(jax.random.randint(streams_of[3], (NBLOCKS,), 1, SB + 1), jax.random.fold_in(streams_of[3], 1), 1, SB).astype(jnp.int32)
    peptide_table = draw_peptide_table(jax.random.fold_in(streams_of[7], 71), 0)
    peptide_bin = draw_peptide_bin(jax.random.fold_in(streams_of[7], 71), 0)
    peptide_shift = jnp.clip(jax.random.uniform(streams_of[6], (PEPTIDES,), jnp.float32, -4.0, 4.0) * block_levels(streams_of[6], (PEPTIDES,), ((0, 64),), -0.4, 0.0), -4.0, 4.0)
    return {"spectra": spectra, "block_start": block_start, "block_range": block_range, "block_count": block_count, "peptide_table": peptide_table, "peptide_bin": peptide_bin, "peptide_shift": peptide_shift}


very_low = -1.0e30
tile_blocks = 32


def reference(spectra, block_start, block_range, block_count, peptide_table, peptide_bin, peptide_shift):
    blocks = spectra.shape[0]
    slab_rows = WIN * PEP_DEV
    table_wide = peptide_table.astype(jnp.float32)
    shift_wide = peptide_shift.astype(jnp.float32)
    order = jnp.argsort(block_start, stable=True).astype(jnp.int32)
    range_ids = jnp.arange(N_MASS, dtype=jnp.int32)
    counts = jnp.sum((block_start[None, :] == range_ids[:, None]).astype(jnp.int32), axis=1).astype(jnp.int32)
    firsts = (jnp.cumsum(counts) - counts).astype(jnp.int32)
    row_ids = jnp.arange(SB, dtype=jnp.int32)
    tile_ids = jnp.arange(tile_blocks, dtype=jnp.int32)

    def one_range(owner, carry):
        begin = (owner * PEP_DEV).astype(jnp.int32)
        rows_table = lax.dynamic_slice_in_dim(table_wide, begin, slab_rows, 0)
        bins = lax.dynamic_slice_in_dim(peptide_bin, begin, slab_rows, 0)
        shifts = lax.dynamic_slice_in_dim(shift_wide, begin, slab_rows, 0)
        first = firsts[owner]
        count = counts[owner]
        trips = ((count + tile_blocks - 1) // tile_blocks).astype(jnp.int32)

        def one_tile(turn, inner):
            lse_all, shift_all, support = inner
            place = (first + turn * tile_blocks + tile_ids).astype(jnp.int32)
            live = place < first + count
            chosen = order[jnp.minimum(place, blocks - 1)]
            block_rows = spectra[chosen].astype(jnp.float32)
            ranges = block_range[chosen]
            filled = block_count[chosen]
            scores = jnp.einsum("tsb,pb->tsp", block_rows, rows_table, precision=lax.Precision.HIGHEST)
            valid = (row_ids[None, :] < filled[:, None]) & live[:, None]
            inside = (bins[None, None, :] >= ranges[:, 0][:, None, None]) & (bins[None, None, :] <= ranges[:, 1][:, None, None]) & valid[:, :, None]
            masked = jnp.where(inside, scores, very_low)
            peak = jnp.max(masked, axis=2)
            weights = jnp.where(inside, jnp.exp(masked - peak[:, :, None]), 0.0)
            denom = jnp.sum(weights, axis=2)
            safe = jnp.where(valid, denom, 1.0)
            lse = jnp.where(valid, peak + jnp.log(safe), 0.0)
            numer = jnp.dot(weights, shifts, precision=lax.Precision.HIGHEST)
            mean_shift = jnp.where(valid, numer / safe, 0.0)
            posterior = jnp.where(inside, jnp.exp(masked - lse[:, :, None]), 0.0)
            current = lax.dynamic_slice_in_dim(support, begin, slab_rows, 0)
            support = lax.dynamic_update_slice_in_dim(support, current + jnp.sum(posterior, axis=(0, 1)), begin, 0)
            target = jnp.where(live, chosen, blocks)
            lse_all = lse_all.at[target].set(lse, mode="drop")
            shift_all = shift_all.at[target].set(mean_shift, mode="drop")
            return (lse_all, shift_all, support)

        return lax.fori_loop(jnp.int32(0), trips, one_tile, carry)

    start_carry = (jnp.zeros((blocks, SB), jnp.float32), jnp.zeros((blocks, SB), jnp.float32), jnp.zeros((N_MASS * PEP_DEV,), jnp.float32))
    lse_all, shift_all, support = lax.fori_loop(jnp.int32(0), jnp.int32(N_MASS - WIN + 1), one_range, start_carry)
    return lse_all, shift_all, support
```

```python
import jax
import jax.numpy as jnp
from jax import lax
from jax.experimental import pallas as pl
from jax.experimental.pallas import tpu as pltpu
from jax.sharding import PartitionSpec as P

SB = 16
LANES = 128
VERY_LOW = -1e30
FLOOR = -1e29
TILE = 256
CHUNK = 512
SUB = 8


def pack_kernel(start_ref, spectra_ref, out_ref, sem):
    blocks = spectra_ref.shape[0]

    def copy(i):
        return pltpu.make_async_copy(spectra_ref.at[i], out_ref.at[start_ref[i]], sem.at[i])

    for i in range(blocks):
        copy(i).start()
    for i in range(blocks):
        copy(i).wait()


def pack_blocks(block_start, spectra, owners):
    blocks, rows, width = spectra.shape
    return pl.pallas_call(
        pack_kernel,
        out_shape=jax.ShapeDtypeStruct((owners, rows, width), spectra.dtype),
        in_specs=[pl.BlockSpec(memory_space=pltpu.SMEM), pl.BlockSpec(memory_space=pltpu.VMEM)],
        out_specs=pl.BlockSpec(memory_space=pl.ANY),
        scratch_shapes=[pltpu.SemaphoreType.DMA((blocks,))],
        compiler_params=pltpu.CompilerParams(vmem_limit_bytes=8 * 1024 * 1024),
        name="pack_blocks",
    )(block_start, spectra)


def after_kernel(*refs):
    pass


def after(value, *tokens):
    return pl.pallas_call(
        after_kernel,
        out_shape=jax.ShapeDtypeStruct(value.shape, value.dtype),
        in_specs=[pl.BlockSpec(memory_space=pl.ANY)] * (1 + len(tokens)),
        out_specs=pl.BlockSpec(memory_space=pl.ANY),
        input_output_aliases={0: 0},
        name="after",
    )(value, *tokens)


def score_kernel(x_hbm, meta_ref, table_ref, bins_ref, shift_ref, ret_ref, sup_ref, x_ref, even_ref, odd_ref, sem):
    tiles = x_ref.shape[0]
    slots = TILE // SB
    chunks = table_ref.shape[0] // CHUNK
    per_chunk = slots // chunks

    def fetch(t):
        return pltpu.make_async_copy(x_hbm.at[pl.ds(t * TILE, TILE)], x_ref.at[t], sem.at[t])

    for t in range(tiles):
        fetch(t).start()
    sup_ref[...] = jnp.zeros_like(sup_ref)
    lane = lax.broadcasted_iota(jnp.int32, (SB, LANES), 1)
    spot = lax.broadcasted_iota(jnp.int32, (SB, LANES), 0)

    def multiply(t, j, into):
        at = pl.ds(pl.multiple_of(j * CHUNK, CHUNK), CHUNK)
        into[:, at] = lax.dot_general(
            x_ref[t], table_ref[at, :], (((1,), (1,)), ((), ())), preferred_element_type=jnp.float32
        )

    def reduce(t, j, source):
        total = None
        for k in range(per_chunk):
            slot = j * per_chunk + k
            parts = []
            for h in range(SB // SUB):
                row = pl.multiple_of(slot * SB + h * SUB, SUB)
                meta_at = pl.ds(pl.multiple_of(t * TILE + row, SUB), SUB)
                lower = meta_ref[meta_at, 0:1]
                upper = meta_ref[meta_at, 1:2]
                bins = bins_ref[...]
                inside = (bins >= lower) & (bins <= upper)
                masked = jnp.where(inside, source[pl.ds(row, SUB), :], VERY_LOW)
                peak = jnp.maximum(jnp.max(masked, axis=1, keepdims=True), FLOOR)
                weights = jnp.exp(masked - peak)
                denom = jnp.sum(weights, axis=1, keepdims=True)
                numer = jnp.sum(weights * shift_ref[...], axis=1, keepdims=True)
                live = denom > 0.0
                safe = jnp.where(live, denom, 1.0)
                inv = jnp.where(live, 1.0 / safe, 0.0)
                mass = weights * inv
                total = mass if total is None else total + mass
                lse = jnp.where(live, peak + jnp.log(safe), 0.0)
                parts.append((lse, numer * inv))
            lse = jnp.concatenate([p[0] for p in parts], axis=0)
            mean = jnp.concatenate([p[1] for p in parts], axis=0)
            flat = jnp.where(lane == spot, lse, jnp.where(lane == spot + SB, mean, 0.0))
            ret_ref[pl.ds(t * slots + slot, 1), :] = jnp.sum(flat, axis=0, keepdims=True)
        sup_ref[...] += total

    for t in range(tiles + 1):
        if t < tiles:
            fetch(t).wait()
        into, source = (even_ref, odd_ref) if t % 2 == 0 else (odd_ref, even_ref)

        def one_chunk(j, carry, t=t, into=into, source=source):
            if t < tiles:
                multiply(t, j, into)
            if t > 0:
                reduce(t - 1, j, source)
            return carry

        lax.fori_loop(0, chunks, one_chunk, 0)


def score_blocks(rows, meta, table, bins, shifts):
    total, width = rows.shape
    wide = table.shape[0]
    vmem = pl.BlockSpec(memory_space=pltpu.VMEM)
    return pl.pallas_call(
        score_kernel,
        out_shape=(
            jax.ShapeDtypeStruct((total // SB, LANES), jnp.float32),
            jax.ShapeDtypeStruct((SUB, wide), jnp.float32),
        ),
        in_specs=[pl.BlockSpec(memory_space=pl.ANY), vmem, vmem, vmem, vmem],
        out_specs=(vmem, vmem),
        scratch_shapes=[
            pltpu.VMEM((total // TILE, TILE, width), rows.dtype),
            pltpu.VMEM((TILE, wide), jnp.float32),
            pltpu.VMEM((TILE, wide), jnp.float32),
            pltpu.SemaphoreType.DMA((total // TILE,)),
        ],
        compiler_params=pltpu.CompilerParams(vmem_limit_bytes=32 * 1024 * 1024),
        cost_estimate=pl.CostEstimate(
            flops=2 * total * width * wide, bytes_accessed=2 * (total + wide) * width, transcendentals=total * wide
        ),
        name="score_blocks",
    )(rows, meta, table, bins, shifts)


def body(spectra, block_start, block_range, block_count, peptide_table, peptide_bin, peptide_shift):
    owners, specs = lax.axis_size("mass"), lax.axis_size("spec")
    spec = lax.axis_index("spec")
    own = peptide_table.shape[0]
    part = own // specs
    back = [((i + 1) % owners, i) for i in range(owners)]
    forth = [(i, (i + 1) % owners) for i in range(owners)]

    quarter = lax.dynamic_slice_in_dim(peptide_table, spec * part, part, 0)
    quarters = [lax.ppermute(quarter, "mass", back)]
    small = jnp.stack([peptide_bin.astype(jnp.float32), peptide_shift])
    next_small = lax.ppermute(small, "mass", back)

    range_ids = jnp.arange(owners, dtype=jnp.int32)
    chosen = block_start[:, None] == range_ids[None, :]
    block_meta = jnp.concatenate([block_range, block_count[:, None]], axis=1)
    meta_out = jnp.sum(jnp.where(chosen[:, :, None], block_meta[:, None, :], 0), axis=0)
    meta_in = lax.all_to_all(meta_out, "mass", split_axis=0, concat_axis=0, tiled=True)

    packed = after(pack_blocks(block_start, spectra, owners), quarters[0], next_small, meta_in)
    received = lax.all_to_all(packed, "mass", split_axis=0, concat_axis=0, tiled=True)

    for k in range(1, specs):
        quarters.append(lax.ppermute(quarters[0], "spec", [(i, (i + k) % specs) for i in range(specs)]))
    pieces = [small] + [
        lax.dynamic_slice_in_dim(next_small, lax.rem(spec + specs - k, specs) * part, part, 1) for k in range(specs)
    ]
    wide_small = jnp.concatenate(pieces, axis=1)
    bins = jnp.broadcast_to(wide_small[0:1], (SUB, 2 * own))
    shifts = jnp.broadcast_to(wide_small[1:2], (SUB, 2 * own))
    table = jnp.concatenate([peptide_table] + quarters, axis=0)

    row_ids = jnp.arange(SB, dtype=jnp.int32)
    valid = row_ids[None, :] < meta_in[:, 2:3]
    lower = jnp.broadcast_to(meta_in[:, 0:1], valid.shape)
    upper = jnp.where(valid, meta_in[:, 1:2], -1)
    row_meta = jnp.stack([lower, upper], axis=2).reshape(owners * SB, 2).astype(jnp.float32)
    row_meta = jnp.pad(row_meta, ((0, 0), (0, LANES - 2)))

    ret, sup = score_blocks(received.reshape(owners * SB, -1), row_meta, table, bins, shifts)

    home = lax.all_to_all(ret, "mass", split_axis=0, concat_axis=0, tiled=True)
    picked = jnp.sum(jnp.where(chosen[:, :, None], home[None, :, : 2 * SB], 0.0), axis=1)
    lse, mean_shift = picked[:, :SB], picked[:, SB:]

    sup = jnp.sum(sup, axis=0).reshape(2, specs, part)
    falling = sup[0, ::-1]
    mine = lax.dynamic_slice_in_dim(jnp.concatenate([falling, falling]), specs - 1 - spec, specs, 0)
    total = jnp.stack([mine[0], sup[1, 0]])
    for k in range(1, specs):
        piece = jnp.stack([mine[k], sup[1, k]])
        total = total + lax.ppermute(piece, "spec", [(i, (i + specs - k) % specs) for i in range(specs)])
    support = total[0] + lax.ppermute(total[1], "mass", forth)
    return (lse, mean_shift, support)


def solution(mesh):
    in_specs = (
        P(("mass", "spec"), None, None),
        P(("mass", "spec")),
        P(("mass", "spec"), None),
        P(("mass", "spec")),
        P("mass", None),
        P("mass"),
        P("mass"),
    )
    out_specs = (P(("mass", "spec"), None), P(("mass", "spec"), None), P(("mass", "spec")))
    return jax.shard_map(body, mesh=mesh, in_specs=in_specs, out_specs=out_specs, check_vma=False)
```

```python
import jax
import jax.numpy as jnp
from jax import lax
from jax.experimental import pallas as pl
from jax.experimental.pallas import tpu as pltpu
from jax.sharding import PartitionSpec as P

SB = 16
GATE_FLOPS = 74_000_000_000
BIN_DEV = 64
LANES = 128
WHOLE_VMEM = 59 * 1024 * 1024
VERY_LOW = -1e30
FLOOR = -1e29
TILE = 256
CHUNK = 512
PAIR = 2
SUB = 8


def pack_kernel(start_ref, range_ref, count_ref, spectra_hbm, out_hbm, held, meta_ref, load_sem, sem, meta_sem):
    blocks, rows, width = held.shape
    batch = blocks // load_sem.shape[0]

    def load(j):
        at = pl.ds(j * batch, batch)
        return pltpu.make_async_copy(spectra_hbm.at[at], held.at[at], load_sem.at[j])

    def copy(i):
        return pltpu.make_async_copy(held.at[i], out_hbm.at[start_ref[i], :, pl.ds(0, width)], sem.at[i])

    for j in range(blocks // batch):
        load(j).start()
    meta_ref[...] = jnp.zeros_like(meta_ref)
    row = lax.broadcasted_iota(jnp.int32, (rows, LANES), 0)
    lane = lax.broadcasted_iota(jnp.int32, (rows, LANES), 1)
    for i in range(blocks):
        first = start_ref[i] * BIN_DEV
        lower = range_ref[0, i] - first
        ends = range_ref[1, i] - first + 1
        value = jnp.where(lane == 0, lower, jnp.where((lane == 1) & (row < count_ref[i]), ends, 0))
        meta_ref[start_ref[i]] = value.astype(jnp.float32).astype(meta_ref.dtype)
    meta_copy = pltpu.make_async_copy(meta_ref, out_hbm.at[:, :, pl.ds(width, LANES)], meta_sem)
    meta_copy.start()
    for j in range(blocks // batch):
        load(j).wait()
        for i in range(j * batch, (j + 1) * batch):
            copy(i).start()
    for i in range(blocks):
        copy(i).wait()
    meta_copy.wait()


def pack_blocks(block_start, block_range, block_count, spectra, owners):
    blocks, rows, width = spectra.shape
    smem = pl.BlockSpec(memory_space=pltpu.SMEM)
    return pl.pallas_call(
        pack_kernel,
        out_shape=jax.ShapeDtypeStruct((owners, rows, width + LANES), spectra.dtype),
        in_specs=[smem, smem, smem, pl.BlockSpec(memory_space=pltpu.HBM)],
        out_specs=pl.BlockSpec(memory_space=pltpu.HBM),
        scratch_shapes=[
            pltpu.VMEM((blocks, rows, width), spectra.dtype),
            pltpu.VMEM((owners, rows, LANES), spectra.dtype),
            pltpu.SemaphoreType.DMA((4,)),
            pltpu.SemaphoreType.DMA((blocks,)),
            pltpu.SemaphoreType.DMA,
        ],
        compiler_params=pltpu.CompilerParams(vmem_limit_bytes=WHOLE_VMEM),
        name="pack_blocks",
    )(block_start, block_range.T, block_count, spectra)


def quarter_kernel(spec_ref, table_hbm, extra_ref, out_hbm, held, load_sem, store_sem, extra_sem):
    part = held.shape[0]
    first = pl.multiple_of(spec_ref[0] * part, part)
    extra = pltpu.make_async_copy(extra_ref, out_hbm.at[pl.ds(part, extra_ref.shape[0])], extra_sem)
    extra.start()
    load = pltpu.make_async_copy(table_hbm.at[pl.ds(first, part)], held, load_sem)
    load.start()
    load.wait()
    store = pltpu.make_async_copy(held, out_hbm.at[pl.ds(0, part)], store_sem)
    store.start()
    store.wait()
    extra.wait()


def cut_quarter(spec, table, extra, part):
    width = table.shape[1]
    hbm = pl.BlockSpec(memory_space=pltpu.HBM)
    return pl.pallas_call(
        quarter_kernel,
        out_shape=jax.ShapeDtypeStruct((part + extra.shape[0], width), table.dtype),
        in_specs=[pl.BlockSpec(memory_space=pltpu.SMEM), hbm, pl.BlockSpec(memory_space=pltpu.VMEM)],
        out_specs=hbm,
        scratch_shapes=[pltpu.VMEM((part, width), table.dtype)] + [pltpu.SemaphoreType.DMA] * 3,
        compiler_params=pltpu.CompilerParams(vmem_limit_bytes=WHOLE_VMEM),
        name="cut_quarter",
    )(spec.reshape(1), table, extra)


def after_kernel(*refs):
    pass


def after(value, *tokens, flops=0):
    hbm = pl.BlockSpec(memory_space=pltpu.HBM)
    return pl.pallas_call(
        after_kernel,
        out_shape=jax.ShapeDtypeStruct(value.shape, value.dtype),
        in_specs=[hbm] * (1 + len(tokens)),
        out_specs=hbm,
        input_output_aliases={0: 0},
        compiler_params=pltpu.CompilerParams(vmem_limit_bytes=WHOLE_VMEM),
        cost_estimate=pl.CostEstimate(flops=flops, bytes_accessed=0, transcendentals=0),
        name="after",
    )(value, *tokens)


def exact_parts(value):
    parts = []
    for _ in range(3):
        top = lax.reduce_precision(value, 8, 7)
        parts.append(top.astype(jnp.bfloat16))
        value = value - top
    return parts


def score_kernel(
    spec_ref, x_hbm, own_hbm, q0_hbm, q1_hbm, q2_hbm, q3_hbm, bins_ref, shift_ref, ret_ref, m0_ref, m1_ref, m2_ref, m3_ref,
    x_ref, table_ref, extra_ref, small_ref, even_ref, odd_ref, held_ref, sum_ref, x_sem, table_sem, small_sem,
):
    tiles = x_ref.shape[0]
    width = table_ref.shape[1]
    slots = TILE // SB
    chunks = table_ref.shape[0] // CHUNK
    part = q0_hbm.shape[0] - SB
    own = own_hbm.shape[0] // part

    def fetch(t):
        return pltpu.make_async_copy(x_hbm.at[pl.ds(t * TILE, TILE)], x_ref.at[t], x_sem.at[t])

    def fetch_part(j):
        source = own_hbm.at[pl.ds(j * part, part)] if j < own else quarters[j - own].at[pl.ds(0, part)]
        return pltpu.make_async_copy(source, table_ref.at[pl.ds(j * part, part)], table_sem.at[j])

    quarters = (q0_hbm, q1_hbm, q2_hbm, q3_hbm)
    smalls = [
        pltpu.make_async_copy(q.at[pl.ds(part, SB)], extra_ref.at[k], small_sem.at[k]) for k, q in enumerate(quarters)
    ]
    parts = table_ref.shape[0] // part
    fetch(0).start()
    for j in range(2 * PAIR):
        fetch_part(j).start()
    sum_ref[...] = jnp.zeros_like(sum_ref)
    lane = lax.broadcasted_iota(jnp.int32, (SUB, LANES), 1)
    spot = lax.broadcasted_iota(jnp.int32, (SUB, LANES), 0)

    def multiply(t, j, into, size=CHUNK):
        at = pl.ds(pl.multiple_of(j * size, size), size)
        into[:, at] = lax.dot_general(
            x_ref[t, :, :width], table_ref[at, :], (((1,), (1,)), ((), ())), preferred_element_type=jnp.float32
        )

    def reduce(t, j, source):
        batch = TILE // chunks
        groups = range(batch // SUB)
        columns = range(source.shape[1] // LANES)
        rows = [pl.ds(pl.multiple_of(j * batch + g * SUB, SUB), SUB) for g in groups]
        here = [slice(g * SUB, (g + 1) * SUB) for g in groups]
        lower, ends = [], []
        for k in range(batch // SB):
            at = pl.ds(pl.multiple_of(j * batch + k * SB, SB), SB)
            meta = x_ref[t, at, width:].astype(jnp.float32)
            for h in range(SB // SUB):
                mine = meta[h * SUB:(h + 1) * SUB]
                lower.append(jnp.broadcast_to(mine[:, 0:1], (SUB, LANES)))
                ends.append(jnp.broadcast_to(mine[:, 1:2], (SUB, LANES)))
        peak = [jnp.full((SUB, LANES), FLOOR, jnp.float32) for g in groups]
        for c in columns:
            at = slice(c * LANES, (c + 1) * LANES)
            bins = jnp.broadcast_to(small_ref[0:1, at], (SUB, LANES))
            for g in groups:
                inside = (bins >= lower[g]) & (bins < ends[g])
                masked = jnp.where(inside, source[rows[g], at], VERY_LOW)
                held_ref[here[g], at] = masked
                peak[g] = jnp.maximum(peak[g], masked)
        peak = [jnp.broadcast_to(jnp.max(p, axis=1, keepdims=True), (SUB, LANES)) for p in peak]
        denom = [jnp.zeros((SUB, LANES), jnp.float32) for g in groups]
        numer = [jnp.zeros((SUB, LANES), jnp.float32) for g in groups]
        for c in columns:
            at = slice(c * LANES, (c + 1) * LANES)
            shift = jnp.broadcast_to(small_ref[1:2, at], (SUB, LANES))
            for g in groups:
                weights = jnp.exp(held_ref[here[g], at] - peak[g])
                held_ref[here[g], at] = weights
                denom[g] = denom[g] + weights
                numer[g] = numer[g] + weights * shift
        denom = [jnp.broadcast_to(jnp.sum(d, axis=1, keepdims=True), (SUB, LANES)) for d in denom]
        numer = [jnp.broadcast_to(jnp.sum(n, axis=1, keepdims=True), (SUB, LANES)) for n in numer]
        live = [d > 0.0 for d in denom]
        safe = [jnp.where(live[g], denom[g], 1.0) for g in groups]
        inv = [jnp.where(live[g], 1.0 / safe[g], 0.0) for g in groups]
        for c in columns:
            at = slice(c * LANES, (c + 1) * LANES)
            total = sum_ref[:, at]
            for g in groups:
                total = total + held_ref[here[g], at] * inv[g]
            sum_ref[:, at] = total
        lse = [jnp.where(live[g], peak[g] + jnp.log(safe[g]), 0.0) for g in groups]
        halves = SB // SUB
        for k in range(batch // SB):
            flat = 0.0
            for h in range(halves):
                g = k * halves + h
                row = spot + h * SUB
                flat = flat + jnp.where(lane == row, lse[g], jnp.where(lane == row + SB, numer[g] * inv[g], 0.0))
            slot = t * slots + j * (batch // SB) + k
            ret_ref[pl.ds(slot, 1), :] = jnp.sum(flat, axis=0, keepdims=True)

    fetch(0).wait()
    for j in range(0, parts, PAIR):
        for k in range(j, j + PAIR):
            fetch_part(k).wait()
        for k in range(j + 2 * PAIR, min(j + 3 * PAIR, parts)):
            fetch_part(k).start()
        if j + 2 * PAIR == parts:
            for copy in smalls:
                copy.start()
            for t in range(1, tiles):
                fetch(t).start()
        multiply(0, j // PAIR, even_ref, PAIR * part)
    small_ref[0:1, :own * part] = bins_ref[...]
    small_ref[1:2, :own * part] = shift_ref[...]
    for k, copy in enumerate(smalls):
        copy.wait()
        extra = extra_ref[k].astype(jnp.float32)[0:1]
        at = slice((own + k) * part, (own + k + 1) * part)
        small_ref[0:1, at] = extra[:, :part] + BIN_DEV
        small_ref[1:2, at] = extra[:, part:2 * part] + extra[:, 2 * part:3 * part] + extra[:, 3 * part:4 * part]

    for t in range(1, tiles + 1):
        if t < tiles:
            fetch(t).wait()
        into, source = (even_ref, odd_ref) if t % 2 == 0 else (odd_ref, even_ref)

        def one_chunk(j, carry, t=t, into=into, source=source):
            if t < tiles:
                multiply(t, j, into)
            reduce(t - 1, j, source)
            return carry

        lax.fori_loop(0, chunks, one_chunk, 0)
    for k, m_ref in enumerate((m0_ref, m1_ref, m2_ref, m3_ref)):
        mine = lax.rem(spec_ref[0] + own - k, own)
        for h, at in enumerate((pl.ds(pl.multiple_of(mine * part, part), part), pl.ds((own + k) * part, part))):
            m_ref[h:h + 1, :] = jnp.sum(sum_ref[:, at], axis=0, keepdims=True)


def score_blocks(spec, rows, table, quarters, bins, shifts):
    total = rows.shape[0]
    wide, width = 2 * table.shape[0], table.shape[1]
    part = quarters[0].shape[0] - SB
    vmem = pl.BlockSpec(memory_space=pltpu.VMEM)
    hbm = pl.BlockSpec(memory_space=pltpu.HBM)
    return pl.pallas_call(
        score_kernel,
        out_shape=(
            jax.ShapeDtypeStruct((total // SB, LANES), jnp.float32),
        )
        + (jax.ShapeDtypeStruct((2, part), jnp.float32),) * len(quarters),
        in_specs=[pl.BlockSpec(memory_space=pltpu.SMEM)] + [hbm] * (2 + len(quarters)) + [vmem, vmem],
        out_specs=(vmem,) * (1 + len(quarters)),
        scratch_shapes=[
            pltpu.VMEM((total // TILE, TILE, rows.shape[1]), rows.dtype),
            pltpu.VMEM((wide, width), table.dtype),
            pltpu.VMEM((len(quarters), SB, width), table.dtype),
            pltpu.VMEM((2, wide), jnp.float32),
            pltpu.VMEM((TILE, wide), jnp.float32),
            pltpu.VMEM((TILE, wide), jnp.float32),
            pltpu.VMEM((TILE * CHUNK // wide, wide), jnp.float32),
            pltpu.VMEM((SUB, wide), jnp.float32),
            pltpu.SemaphoreType.DMA((total // TILE,)),
            pltpu.SemaphoreType.DMA((wide // part,)),
            pltpu.SemaphoreType.DMA((len(quarters),)),
        ],
        compiler_params=pltpu.CompilerParams(vmem_limit_bytes=WHOLE_VMEM),
        cost_estimate=pl.CostEstimate(
            flops=2 * total * width * wide, bytes_accessed=2 * (total + wide) * width, transcendentals=total * wide
        ),
        name="score_blocks",
    )(spec.reshape(1), rows, table, *quarters, bins, shifts)


def body(spectra, block_start, block_range, block_count, peptide_table, peptide_bin, peptide_shift):
    owners, specs = lax.axis_size("mass"), lax.axis_size("spec")
    spec = lax.axis_index("spec")
    own = peptide_table.shape[0]
    part = own // specs
    back = [((i + 1) % owners, i) for i in range(owners)]
    forth = [(i, (i + 1) % owners) for i in range(owners)]

    bins = (peptide_bin - lax.axis_index("mass") * BIN_DEV).astype(jnp.float32)
    values = jnp.stack([bins.astype(jnp.bfloat16)] + exact_parts(peptide_shift)).reshape(4, specs, part)
    extra = lax.dynamic_index_in_dim(values, spec, 1, False).reshape(1, 4 * part)
    extra = jnp.pad(extra, ((0, SB - 1), (0, peptide_table.shape[1] - 4 * part)))
    quarters = [lax.ppermute(cut_quarter(spec, peptide_table, extra, part), "mass", back)]
    packed = pack_blocks(block_start, block_range, block_count, spectra, owners)
    received = lax.all_to_all(packed, "mass", split_axis=0, concat_axis=0, tiled=True)
    for k in range(1, specs):
        quarters.append(lax.ppermute(quarters[0], "spec", [(i, (i + k) % specs) for i in range(specs)]))
    quarters[0] = after(*quarters, flops=GATE_FLOPS)

    ret, *messages = score_blocks(
        spec, received.reshape(owners * SB, -1), peptide_table, quarters, bins[None], peptide_shift[None]
    )

    chosen = block_start[:, None] == jnp.arange(owners, dtype=jnp.int32)[None, :]
    home = lax.all_to_all(ret, "mass", split_axis=0, concat_axis=0, tiled=True)
    picked = jnp.sum(jnp.where(chosen[:, :, None], home[None, :, : 2 * SB], 0.0), axis=1)
    lse, mean_shift = picked[:, :SB], picked[:, SB:]

    total = messages[0]
    for k in range(1, specs):
        total = total + lax.ppermute(messages[k], "spec", [(i, (i + specs - k) % specs) for i in range(specs)])
    support = total[0] + lax.ppermute(total[1], "mass", forth)
    return (lse, mean_shift, support)


def solution(mesh):
    in_specs = (
        P(("mass", "spec"), None, None),
        P(("mass", "spec")),
        P(("mass", "spec"), None),
        P(("mass", "spec")),
        P("mass", None),
        P("mass"),
        P("mass"),
    )
    out_specs = (P(("mass", "spec"), None), P(("mass", "spec"), None), P(("mass", "spec")))
    return jax.shard_map(body, mesh=mesh, in_specs=in_specs, out_specs=out_specs, check_vma=False)
```

```python
import jax
import jax.numpy as jnp
from jax import lax
from jax.experimental import pallas as pl
from jax.experimental.pallas import tpu as pltpu
from jax.sharding import PartitionSpec as P

SB = 16
GATE_FLOPS = 74_000_000_000
PICK_FLOPS = 0
BIN_DEV = 64
LANES = 128
WHOLE_VMEM = 59 * 1024 * 1024
VERY_LOW = -1e30
FLOOR = -1e29
TILE = 256
CHUNK = 512
PAIR = 4
SUB = 8


def prepare_kernel(
    spec_ref, mass_ref, start_ref, range_ref, count_ref, bins_ref, shift_ref, spectra_hbm, table_hbm,
    out_hbm, quarter_hbm, held, meta_ref, part_ref, extra_ref, load_sem, part_sem, sem, tail_sem,
):
    blocks, rows, width = held.shape
    steps = load_sem.shape[0]
    batch, part = blocks // steps, part_ref.shape[0]
    piece = part // steps
    first = pl.multiple_of(spec_ref[0] * part, part)

    def load(j):
        at = pl.ds(j * batch, batch)
        return pltpu.make_async_copy(spectra_hbm.at[at], held.at[at], load_sem.at[j])

    def copy(i):
        return pltpu.make_async_copy(held.at[i], out_hbm.at[start_ref[i], :, pl.ds(0, width)], sem.at[i])

    def load_part(j):
        at = pl.ds(j * piece, piece)
        return pltpu.make_async_copy(table_hbm.at[pl.ds(first + j * piece, piece)], part_ref.at[at], part_sem.at[j])

    def store_part(j):
        at = pl.ds(j * piece, piece)
        return pltpu.make_async_copy(part_ref.at[at], quarter_hbm.at[at], part_sem.at[steps + j])

    for j in range(steps):
        load(j).start()
        load_part(j).start()

    bins = (bins_ref[0:1, pl.ds(first, part)] - mass_ref[0] * BIN_DEV).astype(jnp.float32)
    rest = shift_ref[0:1, pl.ds(first, part)]
    extra_ref[...] = jnp.zeros_like(extra_ref)
    extra_ref[:, :part] = jnp.broadcast_to(bins, (SB, part)).astype(extra_ref.dtype)
    for k in range(1, 4):
        top = jnp.broadcast_to(rest, (SB, part)).astype(extra_ref.dtype)
        extra_ref[:, k * part:(k + 1) * part] = top
        rest = rest - top.astype(jnp.float32)[0:1]
    extra_copy = pltpu.make_async_copy(extra_ref, quarter_hbm.at[pl.ds(part, SB)], tail_sem.at[0])
    extra_copy.start()

    meta_ref[...] = jnp.zeros_like(meta_ref)
    row = lax.broadcasted_iota(jnp.int32, (rows, LANES), 0)
    lane = lax.broadcasted_iota(jnp.int32, (rows, LANES), 1)
    for i in range(blocks):
        low = start_ref[i] * BIN_DEV
        lower = range_ref[0, i] - low
        ends = range_ref[1, i] - low + 1
        value = jnp.where(lane == 0, lower, jnp.where((lane == 1) & (row < count_ref[i]), ends, 0))
        meta_ref[start_ref[i]] = value.astype(jnp.float32).astype(meta_ref.dtype)
    meta_copy = pltpu.make_async_copy(meta_ref, out_hbm.at[:, :, pl.ds(width, LANES)], tail_sem.at[1])
    meta_copy.start()
    for j in range(steps):
        load(j).wait()
        for i in range(j * batch, (j + 1) * batch):
            copy(i).start()
        load_part(j).wait()
        store_part(j).start()
    for i in range(blocks):
        copy(i).wait()
    for j in range(steps):
        store_part(j).wait()
    extra_copy.wait()
    meta_copy.wait()


def prepare(spec, mass, block_start, block_range, block_count, bins, shifts, spectra, table, owners, part):
    blocks, rows, width = spectra.shape
    smem = pl.BlockSpec(memory_space=pltpu.SMEM)
    vmem = pl.BlockSpec(memory_space=pltpu.VMEM)
    hbm = pl.BlockSpec(memory_space=pltpu.HBM)
    steps = 4
    return pl.pallas_call(
        prepare_kernel,
        out_shape=(
            jax.ShapeDtypeStruct((owners, rows, width + LANES), spectra.dtype),
            jax.ShapeDtypeStruct((part + SB, width), table.dtype),
        ),
        in_specs=[smem] * 5 + [vmem] * 2 + [hbm] * 2,
        out_specs=(hbm, hbm),
        scratch_shapes=[
            pltpu.VMEM((blocks, rows, width), spectra.dtype),
            pltpu.VMEM((owners, rows, LANES), spectra.dtype),
            pltpu.VMEM((part, width), table.dtype),
            pltpu.VMEM((SB, width), table.dtype),
            pltpu.SemaphoreType.DMA((steps,)),
            pltpu.SemaphoreType.DMA((2 * steps,)),
            pltpu.SemaphoreType.DMA((blocks,)),
            pltpu.SemaphoreType.DMA((2,)),
        ],
        compiler_params=pltpu.CompilerParams(vmem_limit_bytes=WHOLE_VMEM),
        name="prepare",
    )(
        spec.reshape(1), mass.reshape(1), block_start, block_range.T, block_count, bins[None], shifts[None],
        spectra, table,
    )


def pick_kernel(start_ref, home_ref, lse_ref, mean_ref, rows_ref):
    blocks = lse_ref.shape[1]
    rows_ref[...] = jnp.zeros_like(rows_ref)
    for i in range(blocks):
        rows_ref[i:i + 1, :] = home_ref[pl.ds(start_ref[i], 1), :]
    turned = rows_ref[...].T
    lse_ref[...] = turned[:SB, :blocks]
    mean_ref[...] = turned[SB:2 * SB, :blocks]


def pick(block_start, home):
    blocks = block_start.shape[0]
    out = jax.ShapeDtypeStruct((SB, blocks), home.dtype)
    vmem = pl.BlockSpec(memory_space=pltpu.VMEM)
    lse, mean = pl.pallas_call(
        pick_kernel,
        out_shape=(out, out),
        in_specs=[pl.BlockSpec(memory_space=pltpu.SMEM), vmem],
        out_specs=(vmem, vmem),
        scratch_shapes=[pltpu.VMEM((LANES, LANES), home.dtype)],
        compiler_params=pltpu.CompilerParams(vmem_limit_bytes=4 * 1024 * 1024),
        cost_estimate=pl.CostEstimate(flops=PICK_FLOPS, bytes_accessed=0, transcendentals=0),
        name="pick",
    )(block_start, home)
    return lse.T, mean.T


def after_kernel(*refs):
    pass


def after(value, *tokens, flops=0):
    hbm = pl.BlockSpec(memory_space=pltpu.HBM)
    return pl.pallas_call(
        after_kernel,
        out_shape=jax.ShapeDtypeStruct(value.shape, value.dtype),
        in_specs=[hbm] * (1 + len(tokens)),
        out_specs=hbm,
        input_output_aliases={0: 0},
        compiler_params=pltpu.CompilerParams(vmem_limit_bytes=WHOLE_VMEM),
        cost_estimate=pl.CostEstimate(flops=flops, bytes_accessed=0, transcendentals=0),
        name="after",
    )(value, *tokens)


def score_kernel(
    spec_ref, x_hbm, own_hbm, q0_hbm, q1_hbm, q2_hbm, q3_hbm, bins_ref, shift_ref, ret_ref, m0_ref, m1_ref, m2_ref, m3_ref,
    x_ref, table_ref, extra_ref, small_ref, even_ref, odd_ref, held_ref, sum_ref, x_sem, table_sem, small_sem,
):
    tiles = x_ref.shape[0]
    width = table_ref.shape[1]
    slots = TILE // SB
    chunks = table_ref.shape[0] // CHUNK
    part = q0_hbm.shape[0] - SB
    own = own_hbm.shape[0] // part

    def fetch(t):
        return pltpu.make_async_copy(x_hbm.at[pl.ds(t * TILE, TILE)], x_ref.at[t], x_sem.at[t])

    def fetch_part(j):
        source = own_hbm.at[pl.ds(j * part, part)] if j < own else quarters[j - own].at[pl.ds(0, part)]
        return pltpu.make_async_copy(source, table_ref.at[pl.ds(j * part, part)], table_sem.at[j])

    quarters = (q0_hbm, q1_hbm, q2_hbm, q3_hbm)
    smalls = [
        pltpu.make_async_copy(q.at[pl.ds(part, SB)], extra_ref.at[k], small_sem.at[k]) for k, q in enumerate(quarters)
    ]
    parts = table_ref.shape[0] // part
    fetch(0).start()
    for j in range(own):
        fetch_part(j).start()
    fetch(1).start()
    for j in range(own, parts):
        fetch_part(j).start()
    for copy in smalls:
        copy.start()
    for t in range(2, tiles):
        fetch(t).start()
    sum_ref[...] = jnp.zeros_like(sum_ref)
    lane = lax.broadcasted_iota(jnp.int32, (SUB, LANES), 1)
    spot = lax.broadcasted_iota(jnp.int32, (SUB, LANES), 0)

    def multiply(t, j, into, size=CHUNK):
        at = pl.ds(pl.multiple_of(j * size, size), size)
        into[:, at] = lax.dot_general(
            x_ref[t, :, :width], table_ref[at, :], (((1,), (1,)), ((), ())), preferred_element_type=jnp.float32
        )

    def reduce(t, j, source):
        batch = TILE // chunks
        groups = range(batch // SUB)
        columns = range(source.shape[1] // LANES)
        rows = [pl.ds(pl.multiple_of(j * batch + g * SUB, SUB), SUB) for g in groups]
        here = [slice(g * SUB, (g + 1) * SUB) for g in groups]
        lower, ends = [], []
        for k in range(batch // SB):
            at = pl.ds(pl.multiple_of(j * batch + k * SB, SB), SB)
            meta = x_ref[t, at, width:].astype(jnp.float32)
            for h in range(SB // SUB):
                mine = meta[h * SUB:(h + 1) * SUB]
                lower.append(jnp.broadcast_to(mine[:, 0:1], (SUB, LANES)))
                ends.append(jnp.broadcast_to(mine[:, 1:2], (SUB, LANES)))
        peak = [jnp.full((SUB, LANES), FLOOR, jnp.float32) for g in groups]
        for c in columns:
            at = slice(c * LANES, (c + 1) * LANES)
            bins = jnp.broadcast_to(small_ref[0:1, at], (SUB, LANES))
            for g in groups:
                inside = (bins >= lower[g]) & (bins < ends[g])
                masked = jnp.where(inside, source[rows[g], at], VERY_LOW)
                held_ref[here[g], at] = masked
                peak[g] = jnp.maximum(peak[g], masked)
        peak = [jnp.broadcast_to(jnp.max(p, axis=1, keepdims=True), (SUB, LANES)) for p in peak]
        denom = [jnp.zeros((SUB, LANES), jnp.float32) for g in groups]
        numer = [jnp.zeros((SUB, LANES), jnp.float32) for g in groups]
        for c in columns:
            at = slice(c * LANES, (c + 1) * LANES)
            shift = jnp.broadcast_to(small_ref[1:2, at], (SUB, LANES))
            for g in groups:
                weights = jnp.exp(held_ref[here[g], at] - peak[g])
                held_ref[here[g], at] = weights
                denom[g] = denom[g] + weights
                numer[g] = numer[g] + weights * shift
        denom = [jnp.broadcast_to(jnp.sum(d, axis=1, keepdims=True), (SUB, LANES)) for d in denom]
        numer = [jnp.broadcast_to(jnp.sum(n, axis=1, keepdims=True), (SUB, LANES)) for n in numer]
        live = [d > 0.0 for d in denom]
        safe = [jnp.where(live[g], denom[g], 1.0) for g in groups]
        inv = [jnp.where(live[g], 1.0 / safe[g], 0.0) for g in groups]
        for c in columns:
            at = slice(c * LANES, (c + 1) * LANES)
            total = sum_ref[:, at]
            for g in groups:
                total = total + held_ref[here[g], at] * inv[g]
            sum_ref[:, at] = total
        lse = [jnp.where(live[g], peak[g] + jnp.log(safe[g]), 0.0) for g in groups]
        halves = SB // SUB
        for k in range(batch // SB):
            flat = 0.0
            for h in range(halves):
                g = k * halves + h
                row = spot + h * SUB
                flat = flat + jnp.where(lane == row, lse[g], jnp.where(lane == row + SB, numer[g] * inv[g], 0.0))
            slot = t * slots + j * (batch // SB) + k
            ret_ref[pl.ds(slot, 1), :] = jnp.sum(flat, axis=0, keepdims=True)

    fetch(0).wait()
    for j in range(0, own, PAIR):
        for k in range(j, j + PAIR):
            fetch_part(k).wait()
        multiply(0, j // PAIR, even_ref, PAIR * part)
    fetch(1).wait()
    for j in range(0, own, PAIR):
        multiply(1, j // PAIR, odd_ref, PAIR * part)
    for j in range(own, parts, PAIR):
        for k in range(j, j + PAIR):
            fetch_part(k).wait()
        multiply(0, j // PAIR, even_ref, PAIR * part)
    small_ref[0:1, :own * part] = bins_ref[...]
    small_ref[1:2, :own * part] = shift_ref[...]
    for k, copy in enumerate(smalls):
        copy.wait()
        extra = extra_ref[k].astype(jnp.float32)[0:1]
        at = slice((own + k) * part, (own + k + 1) * part)
        small_ref[0:1, at] = extra[:, :part] + BIN_DEV
        small_ref[1:2, at] = extra[:, part:2 * part] + extra[:, 2 * part:3 * part] + extra[:, 3 * part:4 * part]

    for t in range(1, tiles + 1):
        if 1 < t < tiles:
            fetch(t).wait()
        into, source = (even_ref, odd_ref) if t % 2 == 0 else (odd_ref, even_ref)

        def one_chunk(j, carry, t=t, into=into, source=source):
            if t == 1:
                multiply(t, own + j, into, part)
            elif t < tiles:
                multiply(t, j, into)
            reduce(t - 1, j, source)
            return carry

        lax.fori_loop(0, chunks, one_chunk, 0)
    for k, m_ref in enumerate((m0_ref, m1_ref, m2_ref, m3_ref)):
        mine = lax.rem(spec_ref[0] + own - k, own)
        for h, at in enumerate((pl.ds(pl.multiple_of(mine * part, part), part), pl.ds((own + k) * part, part))):
            m_ref[h:h + 1, :] = jnp.sum(sum_ref[:, at], axis=0, keepdims=True)


def score_blocks(spec, rows, table, quarters, bins, shifts):
    total = rows.shape[0]
    wide, width = 2 * table.shape[0], table.shape[1]
    part = quarters[0].shape[0] - SB
    vmem = pl.BlockSpec(memory_space=pltpu.VMEM)
    hbm = pl.BlockSpec(memory_space=pltpu.HBM)
    return pl.pallas_call(
        score_kernel,
        out_shape=(
            jax.ShapeDtypeStruct((total // SB, LANES), jnp.float32),
        )
        + (jax.ShapeDtypeStruct((2, part), jnp.float32),) * len(quarters),
        in_specs=[pl.BlockSpec(memory_space=pltpu.SMEM)] + [hbm] * (2 + len(quarters)) + [vmem, vmem],
        out_specs=(vmem,) * (1 + len(quarters)),
        scratch_shapes=[
            pltpu.VMEM((total // TILE, TILE, rows.shape[1]), rows.dtype),
            pltpu.VMEM((wide, width), table.dtype),
            pltpu.VMEM((len(quarters), SB, width), table.dtype),
            pltpu.VMEM((2, wide), jnp.float32),
            pltpu.VMEM((TILE, wide), jnp.float32),
            pltpu.VMEM((TILE, wide), jnp.float32),
            pltpu.VMEM((TILE * CHUNK // wide, wide), jnp.float32),
            pltpu.VMEM((SUB, wide), jnp.float32),
            pltpu.SemaphoreType.DMA((total // TILE,)),
            pltpu.SemaphoreType.DMA((wide // part,)),
            pltpu.SemaphoreType.DMA((len(quarters),)),
        ],
        compiler_params=pltpu.CompilerParams(vmem_limit_bytes=WHOLE_VMEM),
        cost_estimate=pl.CostEstimate(
            flops=2 * total * width * wide, bytes_accessed=2 * (total + wide) * width, transcendentals=total * wide
        ),
        name="score_blocks",
    )(spec.reshape(1), rows, table, *quarters, bins, shifts)


def body(spectra, block_start, block_range, block_count, peptide_table, peptide_bin, peptide_shift):
    owners, specs = lax.axis_size("mass"), lax.axis_size("spec")
    spec = lax.axis_index("spec")
    own = peptide_table.shape[0]
    part = own // specs
    back = [((i + 1) % owners, i) for i in range(owners)]
    forth = [(i, (i + 1) % owners) for i in range(owners)]

    mass = lax.axis_index("mass")
    packed, quarter = prepare(
        spec, mass, block_start, block_range, block_count, peptide_bin, peptide_shift, spectra, peptide_table, owners, part
    )
    quarters = [lax.ppermute(quarter, "mass", back)]
    received = lax.all_to_all(packed, "mass", split_axis=0, concat_axis=0, tiled=True)
    for k in range(1, specs):
        quarters.append(lax.ppermute(quarters[0], "spec", [(i, (i + k) % specs) for i in range(specs)]))
    quarters[0] = after(*quarters, flops=GATE_FLOPS)

    bins = (peptide_bin - mass * BIN_DEV).astype(jnp.float32)
    ret, *messages = score_blocks(
        spec, received.reshape(owners * SB, -1), peptide_table, quarters, bins[None], peptide_shift[None]
    )

    home = lax.all_to_all(ret, "mass", split_axis=0, concat_axis=0, tiled=True)
    lse, mean_shift = pick(block_start, home)

    total = messages[0]
    for k in range(1, specs):
        total = total + lax.ppermute(messages[k], "spec", [(i, (i + specs - k) % specs) for i in range(specs)])
    support = total[0] + lax.ppermute(total[1], "mass", forth)
    return (lse, mean_shift, support)


def solution(mesh):
    in_specs = (
        P(("mass", "spec"), None, None),
        P(("mass", "spec")),
        P(("mass", "spec"), None),
        P(("mass", "spec")),
        P("mass", None),
        P("mass"),
        P("mass"),
    )
    out_specs = (P(("mass", "spec"), None), P(("mass", "spec"), None), P(("mass", "spec")))
    return jax.shard_map(body, mesh=mesh, in_specs=in_specs, out_specs=out_specs, check_vma=False)
```

```python
import jax
import jax.numpy as jnp
from jax import lax
from jax.experimental import pallas as pl
from jax.experimental.pallas import tpu as pltpu
from jax.sharding import PartitionSpec as P

SB = 16
GATE_FLOPS = 74_000_000_000
PICK_FLOPS = 0
BIN_DEV = 64
LANES = 128
WHOLE_VMEM = 59 * 1024 * 1024
VERY_LOW = -1e30
FLOOR = -1e29
TILE = 256
CHUNK = 512
PAIR = 4
SUB = 8


def prepare_kernel(
    spec_ref, mass_ref, start_ref, range_ref, count_ref, bins_ref, shift_ref, spectra_hbm, table_hbm,
    out_hbm, quarter_hbm, held, meta_ref, part_ref, extra_ref, load_sem, part_sem, sem, tail_sem,
):
    blocks, rows, width = held.shape
    steps = load_sem.shape[0]
    batch, part = blocks // steps, part_ref.shape[0]
    piece = part // steps
    first = pl.multiple_of(spec_ref[0] * part, part)

    def load(j):
        at = pl.ds(j * batch, batch)
        return pltpu.make_async_copy(spectra_hbm.at[at], held.at[at], load_sem.at[j])

    def copy(i):
        return pltpu.make_async_copy(held.at[i], out_hbm.at[start_ref[i], :, pl.ds(0, width)], sem.at[i])

    def load_part(j):
        at = pl.ds(j * piece, piece)
        return pltpu.make_async_copy(table_hbm.at[pl.ds(first + j * piece, piece)], part_ref.at[at], part_sem.at[j])

    def store_part(j):
        at = pl.ds(j * piece, piece)
        return pltpu.make_async_copy(part_ref.at[at], quarter_hbm.at[at], part_sem.at[steps + j])

    for j in range(steps):
        load(j).start()
        load_part(j).start()

    bins = (bins_ref[0:1, pl.ds(first, part)] - mass_ref[0] * BIN_DEV).astype(jnp.float32)
    rest = shift_ref[0:1, pl.ds(first, part)]
    extra_ref[...] = jnp.zeros_like(extra_ref)
    extra_ref[:, :part] = jnp.broadcast_to(bins, (SB, part)).astype(extra_ref.dtype)
    for k in range(1, 4):
        top = jnp.broadcast_to(rest, (SB, part)).astype(extra_ref.dtype)
        extra_ref[:, k * part:(k + 1) * part] = top
        rest = rest - top.astype(jnp.float32)[0:1]
    extra_copy = pltpu.make_async_copy(extra_ref, quarter_hbm.at[pl.ds(part, SB)], tail_sem.at[0])
    extra_copy.start()

    meta_ref[...] = jnp.zeros_like(meta_ref)
    row = lax.broadcasted_iota(jnp.int32, (rows, LANES), 0)
    lane = lax.broadcasted_iota(jnp.int32, (rows, LANES), 1)
    for i in range(blocks):
        low = start_ref[i] * BIN_DEV
        lower = range_ref[0, i] - low
        ends = range_ref[1, i] - low + 1
        value = jnp.where(lane == 0, lower, jnp.where((lane == 1) & (row < count_ref[i]), ends, 0))
        meta_ref[start_ref[i]] = value.astype(jnp.float32).astype(meta_ref.dtype)
    meta_copy = pltpu.make_async_copy(meta_ref, out_hbm.at[:, :, pl.ds(width, LANES)], tail_sem.at[1])
    meta_copy.start()
    for j in range(steps):
        load(j).wait()
        for i in range(j * batch, (j + 1) * batch):
            copy(i).start()
        load_part(j).wait()
        store_part(j).start()
    for i in range(blocks):
        copy(i).wait()
    for j in range(steps):
        store_part(j).wait()
    extra_copy.wait()
    meta_copy.wait()


def prepare(spec, mass, block_start, block_range, block_count, bins, shifts, spectra, table, owners, part):
    blocks, rows, width = spectra.shape
    smem = pl.BlockSpec(memory_space=pltpu.SMEM)
    vmem = pl.BlockSpec(memory_space=pltpu.VMEM)
    hbm = pl.BlockSpec(memory_space=pltpu.HBM)
    steps = 4
    return pl.pallas_call(
        prepare_kernel,
        out_shape=(
            jax.ShapeDtypeStruct((owners, rows, width + LANES), spectra.dtype),
            jax.ShapeDtypeStruct((part + SB, width), table.dtype),
        ),
        in_specs=[smem] * 5 + [vmem] * 2 + [hbm] * 2,
        out_specs=(hbm, hbm),
        scratch_shapes=[
            pltpu.VMEM((blocks, rows, width), spectra.dtype),
            pltpu.VMEM((owners, rows, LANES), spectra.dtype),
            pltpu.VMEM((part, width), table.dtype),
            pltpu.VMEM((SB, width), table.dtype),
            pltpu.SemaphoreType.DMA((steps,)),
            pltpu.SemaphoreType.DMA((2 * steps,)),
            pltpu.SemaphoreType.DMA((blocks,)),
            pltpu.SemaphoreType.DMA((2,)),
        ],
        compiler_params=pltpu.CompilerParams(vmem_limit_bytes=WHOLE_VMEM),
        name="prepare",
    )(
        spec.reshape(1), mass.reshape(1), block_start, block_range.T, block_count, bins[None], shifts[None],
        spectra, table,
    )


def pick_kernel(start_ref, home_ref, lse_ref, mean_ref, rows_ref):
    blocks = lse_ref.shape[1]
    rows_ref[...] = jnp.zeros_like(rows_ref)
    for i in range(blocks):
        rows_ref[i:i + 1, :] = home_ref[pl.ds(start_ref[i], 1), :]
    turned = rows_ref[...].T
    lse_ref[...] = turned[:SB, :blocks]
    mean_ref[...] = turned[SB:2 * SB, :blocks]


def pick(block_start, home):
    blocks = block_start.shape[0]
    out = jax.ShapeDtypeStruct((SB, blocks), home.dtype)
    vmem = pl.BlockSpec(memory_space=pltpu.VMEM)
    lse, mean = pl.pallas_call(
        pick_kernel,
        out_shape=(out, out),
        in_specs=[pl.BlockSpec(memory_space=pltpu.SMEM), vmem],
        out_specs=(vmem, vmem),
        scratch_shapes=[pltpu.VMEM((LANES, LANES), home.dtype)],
        compiler_params=pltpu.CompilerParams(vmem_limit_bytes=4 * 1024 * 1024),
        cost_estimate=pl.CostEstimate(flops=PICK_FLOPS, bytes_accessed=0, transcendentals=0),
        name="pick",
    )(block_start, home)
    return lse.T, mean.T


def after_kernel(*refs):
    pass


def after(value, *tokens, flops=0):
    hbm = pl.BlockSpec(memory_space=pltpu.HBM)
    return pl.pallas_call(
        after_kernel,
        out_shape=jax.ShapeDtypeStruct(value.shape, value.dtype),
        in_specs=[hbm] * (1 + len(tokens)),
        out_specs=hbm,
        input_output_aliases={0: 0},
        compiler_params=pltpu.CompilerParams(vmem_limit_bytes=WHOLE_VMEM),
        cost_estimate=pl.CostEstimate(flops=flops, bytes_accessed=0, transcendentals=0),
        name="after",
    )(value, *tokens)


def score_kernel(
    spec_ref, x_hbm, own_hbm, q0_hbm, q1_hbm, q2_hbm, q3_hbm, bins_ref, shift_ref, ret_ref, mine_ref, next_ref,
    x_ref, table_ref, extra_ref, small_ref, even_ref, odd_ref, held_ref, sum_ref, x_sem, table_sem, small_sem,
):
    tiles = x_ref.shape[0]
    width = table_ref.shape[1]
    slots = TILE // SB
    chunks = table_ref.shape[0] // CHUNK
    part = q0_hbm.shape[0] - SB
    own = own_hbm.shape[0] // part

    def fetch(t):
        return pltpu.make_async_copy(x_hbm.at[pl.ds(t * TILE, TILE)], x_ref.at[t], x_sem.at[t])

    def fetch_part(j):
        source = own_hbm.at[pl.ds(j * part, part)] if j < own else quarters[j - own].at[pl.ds(0, part)]
        return pltpu.make_async_copy(source, table_ref.at[pl.ds(j * part, part)], table_sem.at[j])

    quarters = (q0_hbm, q1_hbm, q2_hbm, q3_hbm)
    smalls = [
        pltpu.make_async_copy(q.at[pl.ds(part, SB)], extra_ref.at[k], small_sem.at[k]) for k, q in enumerate(quarters)
    ]
    parts = table_ref.shape[0] // part
    fetch(0).start()
    for j in range(own):
        fetch_part(j).start()
    fetch(1).start()
    for j in range(own, parts):
        fetch_part(j).start()
    for copy in smalls:
        copy.start()
    for t in range(2, tiles):
        fetch(t).start()
    sum_ref[...] = jnp.zeros_like(sum_ref)
    lane = lax.broadcasted_iota(jnp.int32, (SUB, LANES), 1)
    spot = lax.broadcasted_iota(jnp.int32, (SUB, LANES), 0)

    def multiply(t, j, into, size=CHUNK):
        at = pl.ds(pl.multiple_of(j * size, size), size)
        into[:, at] = lax.dot_general(
            x_ref[t, :, :width], table_ref[at, :], (((1,), (1,)), ((), ())), preferred_element_type=jnp.float32
        )

    def reduce(t, j, source):
        batch = TILE // chunks
        groups = range(batch // SUB)
        columns = range(source.shape[1] // LANES)
        rows = [pl.ds(pl.multiple_of(j * batch + g * SUB, SUB), SUB) for g in groups]
        here = [slice(g * SUB, (g + 1) * SUB) for g in groups]
        lower, ends = [], []
        for k in range(batch // SB):
            at = pl.ds(pl.multiple_of(j * batch + k * SB, SB), SB)
            meta = x_ref[t, at, width:].astype(jnp.float32)
            for h in range(SB // SUB):
                mine = meta[h * SUB:(h + 1) * SUB]
                lower.append(jnp.broadcast_to(mine[:, 0:1], (SUB, LANES)))
                ends.append(jnp.broadcast_to(mine[:, 1:2], (SUB, LANES)))
        peak = [jnp.full((SUB, LANES), FLOOR, jnp.float32) for g in groups]
        for c in columns:
            at = slice(c * LANES, (c + 1) * LANES)
            bins = jnp.broadcast_to(small_ref[0:1, at], (SUB, LANES))
            for g in groups:
                inside = (bins >= lower[g]) & (bins < ends[g])
                masked = jnp.where(inside, source[rows[g], at], VERY_LOW)
                held_ref[here[g], at] = masked
                peak[g] = jnp.maximum(peak[g], masked)
        peak = [jnp.broadcast_to(jnp.max(p, axis=1, keepdims=True), (SUB, LANES)) for p in peak]
        denom = [jnp.zeros((SUB, LANES), jnp.float32) for g in groups]
        numer = [jnp.zeros((SUB, LANES), jnp.float32) for g in groups]
        for c in columns:
            at = slice(c * LANES, (c + 1) * LANES)
            shift = jnp.broadcast_to(small_ref[1:2, at], (SUB, LANES))
            for g in groups:
                weights = jnp.exp(held_ref[here[g], at] - peak[g])
                held_ref[here[g], at] = weights
                denom[g] = denom[g] + weights
                numer[g] = numer[g] + weights * shift
        denom = [jnp.broadcast_to(jnp.sum(d, axis=1, keepdims=True), (SUB, LANES)) for d in denom]
        numer = [jnp.broadcast_to(jnp.sum(n, axis=1, keepdims=True), (SUB, LANES)) for n in numer]
        live = [d > 0.0 for d in denom]
        safe = [jnp.where(live[g], denom[g], 1.0) for g in groups]
        inv = [jnp.where(live[g], 1.0 / safe[g], 0.0) for g in groups]
        for c in columns:
            at = slice(c * LANES, (c + 1) * LANES)
            total = sum_ref[:, at]
            for g in groups:
                total = total + held_ref[here[g], at] * inv[g]
            sum_ref[:, at] = total
        lse = [jnp.where(live[g], peak[g] + jnp.log(safe[g]), 0.0) for g in groups]
        halves = SB // SUB
        for k in range(batch // SB):
            flat = 0.0
            for h in range(halves):
                g = k * halves + h
                row = spot + h * SUB
                flat = flat + jnp.where(lane == row, lse[g], jnp.where(lane == row + SB, numer[g] * inv[g], 0.0))
            slot = t * slots + j * (batch // SB) + k
            ret_ref[pl.ds(slot, 1), :] = jnp.sum(flat, axis=0, keepdims=True)

    fetch(0).wait()
    for j in range(0, own, PAIR):
        for k in range(j, j + PAIR):
            fetch_part(k).wait()
        multiply(0, j // PAIR, even_ref, PAIR * part)
    fetch(1).wait()
    for j in range(0, own, PAIR):
        multiply(1, j // PAIR, odd_ref, PAIR * part)
    for j in range(own, parts, PAIR):
        for k in range(j, j + PAIR):
            fetch_part(k).wait()
        multiply(0, j // PAIR, even_ref, PAIR * part)
    small_ref[0:1, :own * part] = bins_ref[...]
    small_ref[1:2, :own * part] = shift_ref[...]
    for k, copy in enumerate(smalls):
        copy.wait()
        extra = extra_ref[k].astype(jnp.float32)[0:1]
        at = slice((own + k) * part, (own + k + 1) * part)
        small_ref[0:1, at] = extra[:, :part] + BIN_DEV
        small_ref[1:2, at] = extra[:, part:2 * part] + extra[:, 2 * part:3 * part] + extra[:, 3 * part:4 * part]

    for t in range(1, tiles + 1):
        if 1 < t < tiles:
            fetch(t).wait()
        into, source = (even_ref, odd_ref) if t % 2 == 0 else (odd_ref, even_ref)

        def one_chunk(j, carry, t=t, into=into, source=source):
            if t == 1:
                multiply(t, own + j, into, part)
            elif t < tiles:
                multiply(t, j, into)
            reduce(t - 1, j, source)
            return carry

        lax.fori_loop(0, chunks, one_chunk, 0)
    for k in range(own):
        here, there = slice(k * part, (k + 1) * part), slice((own + k) * part, (own + k + 1) * part)
        mine_ref[k:k + 1, :] = jnp.sum(sum_ref[:, here], axis=0, keepdims=True)
        held_quarter = lax.rem(spec_ref[0] + own - k, own)
        next_ref[pl.ds(held_quarter, 1), :] = jnp.sum(sum_ref[:, there], axis=0, keepdims=True)


def score_blocks(spec, rows, table, quarters, bins, shifts):
    total = rows.shape[0]
    wide, width = 2 * table.shape[0], table.shape[1]
    part = quarters[0].shape[0] - SB
    vmem = pl.BlockSpec(memory_space=pltpu.VMEM)
    hbm = pl.BlockSpec(memory_space=pltpu.HBM)
    return pl.pallas_call(
        score_kernel,
        out_shape=(
            jax.ShapeDtypeStruct((total // SB, LANES), jnp.float32),
        )
        + (jax.ShapeDtypeStruct((len(quarters), part), jnp.float32),) * 2,
        in_specs=[pl.BlockSpec(memory_space=pltpu.SMEM)] + [hbm] * (2 + len(quarters)) + [vmem, vmem],
        out_specs=(vmem,) * 3,
        scratch_shapes=[
            pltpu.VMEM((total // TILE, TILE, rows.shape[1]), rows.dtype),
            pltpu.VMEM((wide, width), table.dtype),
            pltpu.VMEM((len(quarters), SB, width), table.dtype),
            pltpu.VMEM((2, wide), jnp.float32),
            pltpu.VMEM((TILE, wide), jnp.float32),
            pltpu.VMEM((TILE, wide), jnp.float32),
            pltpu.VMEM((TILE * CHUNK // wide, wide), jnp.float32),
            pltpu.VMEM((SUB, wide), jnp.float32),
            pltpu.SemaphoreType.DMA((total // TILE,)),
            pltpu.SemaphoreType.DMA((wide // part,)),
            pltpu.SemaphoreType.DMA((len(quarters),)),
        ],
        compiler_params=pltpu.CompilerParams(vmem_limit_bytes=WHOLE_VMEM),
        cost_estimate=pl.CostEstimate(
            flops=2 * total * width * wide, bytes_accessed=2 * (total + wide) * width, transcendentals=total * wide
        ),
        name="score_blocks",
    )(spec.reshape(1), rows, table, *quarters, bins, shifts)


def body(spectra, block_start, block_range, block_count, peptide_table, peptide_bin, peptide_shift):
    owners, specs = lax.axis_size("mass"), lax.axis_size("spec")
    spec = lax.axis_index("spec")
    own = peptide_table.shape[0]
    part = own // specs
    back = [((i + 1) % owners, i) for i in range(owners)]
    forth = [(i, (i + 1) % owners) for i in range(owners)]

    mass = lax.axis_index("mass")
    packed, quarter = prepare(
        spec, mass, block_start, block_range, block_count, peptide_bin, peptide_shift, spectra, peptide_table, owners, part
    )
    quarters = [lax.ppermute(quarter, "mass", back)]
    received = lax.all_to_all(packed, "mass", split_axis=0, concat_axis=0, tiled=True)
    for k in range(1, specs):
        quarters.append(lax.ppermute(quarters[0], "spec", [(i, (i + k) % specs) for i in range(specs)]))
    quarters[0] = after(*quarters, flops=GATE_FLOPS)

    bins = (peptide_bin - mass * BIN_DEV).astype(jnp.float32)
    ret, mine, after_mine = score_blocks(
        spec, received.reshape(owners * SB, -1), peptide_table, quarters, bins[None], peptide_shift[None]
    )

    home = lax.all_to_all(ret, "mass", split_axis=0, concat_axis=0, tiled=True)
    lse, mean_shift = pick(block_start, home)

    total = mine + lax.ppermute(after_mine, "mass", forth)
    support = lax.dynamic_index_in_dim(lax.psum(total, "spec"), spec, 0, False)
    return (lse, mean_shift, support)


def solution(mesh):
    in_specs = (
        P(("mass", "spec"), None, None),
        P(("mass", "spec")),
        P(("mass", "spec"), None),
        P(("mass", "spec")),
        P("mass", None),
        P("mass"),
        P("mass"),
    )
    out_specs = (P(("mass", "spec"), None), P(("mass", "spec"), None), P(("mass", "spec")))
    return jax.shard_map(body, mesh=mesh, in_specs=in_specs, out_specs=out_specs, check_vma=False)
```

```python
import jax
import jax.numpy as jnp
from jax import lax
from jax.experimental import pallas as pl
from jax.experimental.pallas import tpu as pltpu
from jax.sharding import PartitionSpec as P

SB = 16
GATE_FLOPS = 74_000_000_000
PICK_FLOPS = 0
BIN_DEV = 64
LANES = 128
WHOLE_VMEM = 59 * 1024 * 1024
VERY_LOW = -1e30
FLOOR = -1e29
TILE = 256
CHUNK = 512
PAIR = 4
SUB = 8


def cut_kernel(spec_ref, mass_ref, bins_ref, shift_ref, table_hbm, quarter_hbm, part_ref, extra_ref, load_sem, store_sem, sem):
    steps, part = load_sem.shape[0], part_ref.shape[0]
    piece = part // steps
    first = pl.multiple_of(spec_ref[0] * part, part)

    def load(j):
        at = pl.ds(j * piece, piece)
        return pltpu.make_async_copy(table_hbm.at[pl.ds(first + j * piece, piece)], part_ref.at[at], load_sem.at[j])

    def store(j):
        at = pl.ds(j * piece, piece)
        return pltpu.make_async_copy(part_ref.at[at], quarter_hbm.at[at], store_sem.at[j])

    for j in range(steps):
        load(j).start()
    bins = (bins_ref[0:1, pl.ds(first, part)] - mass_ref[0] * BIN_DEV).astype(jnp.float32)
    rest = shift_ref[0:1, pl.ds(first, part)]
    extra_ref[...] = jnp.zeros_like(extra_ref)
    extra_ref[:, :part] = jnp.broadcast_to(bins, (SB, part)).astype(extra_ref.dtype)
    for k in range(1, 4):
        top = jnp.broadcast_to(rest, (SB, part)).astype(extra_ref.dtype)
        extra_ref[:, k * part:(k + 1) * part] = top
        rest = rest - top.astype(jnp.float32)[0:1]
    extra_copy = pltpu.make_async_copy(extra_ref, quarter_hbm.at[pl.ds(part, SB)], sem)
    extra_copy.start()
    for j in range(steps):
        load(j).wait()
        store(j).start()
    for j in range(steps):
        store(j).wait()
    extra_copy.wait()


def cut_quarter(spec, mass, bins, shifts, table, part):
    width = table.shape[1]
    smem = pl.BlockSpec(memory_space=pltpu.SMEM)
    vmem = pl.BlockSpec(memory_space=pltpu.VMEM)
    hbm = pl.BlockSpec(memory_space=pltpu.HBM)
    steps = 4
    return pl.pallas_call(
        cut_kernel,
        out_shape=jax.ShapeDtypeStruct((part + SB, width), table.dtype),
        in_specs=[smem, smem, vmem, vmem, hbm],
        out_specs=hbm,
        scratch_shapes=[
            pltpu.VMEM((part, width), table.dtype),
            pltpu.VMEM((SB, width), table.dtype),
            pltpu.SemaphoreType.DMA((steps,)),
            pltpu.SemaphoreType.DMA((steps,)),
            pltpu.SemaphoreType.DMA,
        ],
        compiler_params=pltpu.CompilerParams(vmem_limit_bytes=WHOLE_VMEM),
        name="cut_quarter",
    )(spec.reshape(1), mass.reshape(1), bins[None], shifts[None], table)


def pack_kernel(start_ref, range_ref, count_ref, spectra_hbm, out_hbm, held, meta_ref, load_sem, sem, meta_sem):
    blocks, rows, width = held.shape
    batch = blocks // load_sem.shape[0]

    def load(j):
        at = pl.ds(j * batch, batch)
        return pltpu.make_async_copy(spectra_hbm.at[at], held.at[at], load_sem.at[j])

    def copy(i):
        return pltpu.make_async_copy(held.at[i], out_hbm.at[start_ref[i], :, pl.ds(0, width)], sem.at[i])

    for j in range(blocks // batch):
        load(j).start()
    meta_ref[...] = jnp.zeros_like(meta_ref)
    row = lax.broadcasted_iota(jnp.int32, (rows, LANES), 0)
    lane = lax.broadcasted_iota(jnp.int32, (rows, LANES), 1)
    for i in range(blocks):
        low = start_ref[i] * BIN_DEV
        lower = range_ref[0, i] - low
        ends = range_ref[1, i] - low + 1
        value = jnp.where(lane == 0, lower, jnp.where((lane == 1) & (row < count_ref[i]), ends, 0))
        meta_ref[start_ref[i]] = value.astype(jnp.float32).astype(meta_ref.dtype)
    meta_copy = pltpu.make_async_copy(meta_ref, out_hbm.at[:, :, pl.ds(width, LANES)], meta_sem)
    meta_copy.start()
    for j in range(blocks // batch):
        load(j).wait()
        for i in range(j * batch, (j + 1) * batch):
            copy(i).start()
    for i in range(blocks):
        copy(i).wait()
    meta_copy.wait()


def pack_blocks(block_start, block_range, block_count, spectra, owners):
    blocks, rows, width = spectra.shape
    smem = pl.BlockSpec(memory_space=pltpu.SMEM)
    hbm = pl.BlockSpec(memory_space=pltpu.HBM)
    return pl.pallas_call(
        pack_kernel,
        out_shape=jax.ShapeDtypeStruct((owners, rows, width + LANES), spectra.dtype),
        in_specs=[smem, smem, smem, hbm],
        out_specs=hbm,
        scratch_shapes=[
            pltpu.VMEM((blocks, rows, width), spectra.dtype),
            pltpu.VMEM((owners, rows, LANES), spectra.dtype),
            pltpu.SemaphoreType.DMA((4,)),
            pltpu.SemaphoreType.DMA((blocks,)),
            pltpu.SemaphoreType.DMA,
        ],
        compiler_params=pltpu.CompilerParams(vmem_limit_bytes=WHOLE_VMEM),
        name="pack_blocks",
    )(block_start, block_range.T, block_count, spectra)


def pick_kernel(start_ref, home_ref, lse_ref, mean_ref, rows_ref):
    blocks = lse_ref.shape[1]
    rows_ref[...] = jnp.zeros_like(rows_ref)
    for i in range(blocks):
        rows_ref[i:i + 1, :] = home_ref[pl.ds(start_ref[i], 1), :]
    turned = rows_ref[...].T
    lse_ref[...] = turned[:SB, :blocks]
    mean_ref[...] = turned[SB:2 * SB, :blocks]


def pick(block_start, home):
    blocks = block_start.shape[0]
    out = jax.ShapeDtypeStruct((SB, blocks), home.dtype)
    vmem = pl.BlockSpec(memory_space=pltpu.VMEM)
    lse, mean = pl.pallas_call(
        pick_kernel,
        out_shape=(out, out),
        in_specs=[pl.BlockSpec(memory_space=pltpu.SMEM), vmem],
        out_specs=(vmem, vmem),
        scratch_shapes=[pltpu.VMEM((LANES, LANES), home.dtype)],
        compiler_params=pltpu.CompilerParams(vmem_limit_bytes=4 * 1024 * 1024),
        cost_estimate=pl.CostEstimate(flops=PICK_FLOPS, bytes_accessed=0, transcendentals=0),
        name="pick",
    )(block_start, home)
    return lse.T, mean.T


def after_kernel(*refs):
    pass


def after(value, *tokens, flops=0):
    hbm = pl.BlockSpec(memory_space=pltpu.HBM)
    return pl.pallas_call(
        after_kernel,
        out_shape=jax.ShapeDtypeStruct(value.shape, value.dtype),
        in_specs=[hbm] * (1 + len(tokens)),
        out_specs=hbm,
        input_output_aliases={0: 0},
        compiler_params=pltpu.CompilerParams(vmem_limit_bytes=WHOLE_VMEM),
        cost_estimate=pl.CostEstimate(flops=flops, bytes_accessed=0, transcendentals=0),
        name="after",
    )(value, *tokens)


def score_kernel(
    spec_ref, x_hbm, own_hbm, q0_hbm, q1_hbm, q2_hbm, q3_hbm, bins_ref, shift_ref, ret_ref, mine_ref, next_ref,
    x_ref, table_ref, extra_ref, small_ref, even_ref, odd_ref, held_ref, sum_ref, x_sem, table_sem, small_sem,
):
    tiles = x_ref.shape[0]
    width = table_ref.shape[1]
    slots = TILE // SB
    chunks = table_ref.shape[0] // CHUNK
    part = q0_hbm.shape[0] - SB
    own = own_hbm.shape[0] // part

    def fetch(t):
        return pltpu.make_async_copy(x_hbm.at[pl.ds(t * TILE, TILE)], x_ref.at[t], x_sem.at[t])

    def fetch_part(j):
        source = own_hbm.at[pl.ds(j * part, part)] if j < own else quarters[j - own].at[pl.ds(0, part)]
        return pltpu.make_async_copy(source, table_ref.at[pl.ds(j * part, part)], table_sem.at[j])

    quarters = (q0_hbm, q1_hbm, q2_hbm, q3_hbm)
    smalls = [
        pltpu.make_async_copy(q.at[pl.ds(part, SB)], extra_ref.at[k], small_sem.at[k]) for k, q in enumerate(quarters)
    ]
    parts = table_ref.shape[0] // part
    fetch(0).start()
    for j in range(own):
        fetch_part(j).start()
    fetch(1).start()
    for j in range(own, parts):
        fetch_part(j).start()
    for copy in smalls:
        copy.start()
    for t in range(2, tiles):
        fetch(t).start()
    sum_ref[...] = jnp.zeros_like(sum_ref)
    lane = lax.broadcasted_iota(jnp.int32, (SUB, LANES), 1)
    spot = lax.broadcasted_iota(jnp.int32, (SUB, LANES), 0)

    def multiply(t, j, into, size=CHUNK):
        at = pl.ds(pl.multiple_of(j * size, size), size)
        into[:, at] = lax.dot_general(
            x_ref[t, :, :width], table_ref[at, :], (((1,), (1,)), ((), ())), preferred_element_type=jnp.float32
        )

    def reduce(t, j, source):
        batch = TILE // chunks
        groups = range(batch // SUB)
        columns = range(source.shape[1] // LANES)
        rows = [pl.ds(pl.multiple_of(j * batch + g * SUB, SUB), SUB) for g in groups]
        here = [slice(g * SUB, (g + 1) * SUB) for g in groups]
        lower, ends = [], []
        for k in range(batch // SB):
            at = pl.ds(pl.multiple_of(j * batch + k * SB, SB), SB)
            meta = x_ref[t, at, width:].astype(jnp.float32)
            for h in range(SB // SUB):
                mine = meta[h * SUB:(h + 1) * SUB]
                lower.append(jnp.broadcast_to(mine[:, 0:1], (SUB, LANES)))
                ends.append(jnp.broadcast_to(mine[:, 1:2], (SUB, LANES)))
        peak = [jnp.full((SUB, LANES), FLOOR, jnp.float32) for g in groups]
        for c in columns:
            at = slice(c * LANES, (c + 1) * LANES)
            bins = jnp.broadcast_to(small_ref[0:1, at], (SUB, LANES))
            for g in groups:
                inside = (bins >= lower[g]) & (bins < ends[g])
                masked = jnp.where(inside, source[rows[g], at], VERY_LOW)
                held_ref[here[g], at] = masked
                peak[g] = jnp.maximum(peak[g], masked)
        peak = [jnp.broadcast_to(jnp.max(p, axis=1, keepdims=True), (SUB, LANES)) for p in peak]
        denom = [jnp.zeros((SUB, LANES), jnp.float32) for g in groups]
        numer = [jnp.zeros((SUB, LANES), jnp.float32) for g in groups]
        for c in columns:
            at = slice(c * LANES, (c + 1) * LANES)
            shift = jnp.broadcast_to(small_ref[1:2, at], (SUB, LANES))
            for g in groups:
                weights = jnp.exp(held_ref[here[g], at] - peak[g])
                held_ref[here[g], at] = weights
                denom[g] = denom[g] + weights
                numer[g] = numer[g] + weights * shift
        denom = [jnp.broadcast_to(jnp.sum(d, axis=1, keepdims=True), (SUB, LANES)) for d in denom]
        numer = [jnp.broadcast_to(jnp.sum(n, axis=1, keepdims=True), (SUB, LANES)) for n in numer]
        live = [d > 0.0 for d in denom]
        safe = [jnp.where(live[g], denom[g], 1.0) for g in groups]
        inv = [jnp.where(live[g], 1.0 / safe[g], 0.0) for g in groups]
        for c in columns:
            at = slice(c * LANES, (c + 1) * LANES)
            total = sum_ref[:, at]
            for g in groups:
                total = total + held_ref[here[g], at] * inv[g]
            sum_ref[:, at] = total
        lse = [jnp.where(live[g], peak[g] + jnp.log(safe[g]), 0.0) for g in groups]
        halves = SB // SUB
        for k in range(batch // SB):
            flat = 0.0
            for h in range(halves):
                g = k * halves + h
                row = spot + h * SUB
                flat = flat + jnp.where(lane == row, lse[g], jnp.where(lane == row + SB, numer[g] * inv[g], 0.0))
            slot = t * slots + j * (batch // SB) + k
            ret_ref[pl.ds(slot, 1), :] = jnp.sum(flat, axis=0, keepdims=True)

    fetch(0).wait()
    for j in range(0, own, PAIR):
        for k in range(j, j + PAIR):
            fetch_part(k).wait()
        multiply(0, j // PAIR, even_ref, PAIR * part)
    fetch(1).wait()
    for j in range(0, own, PAIR):
        multiply(1, j // PAIR, odd_ref, PAIR * part)
    for j in range(own, parts, PAIR):
        for k in range(j, j + PAIR):
            fetch_part(k).wait()
        multiply(0, j // PAIR, even_ref, PAIR * part)
    small_ref[0:1, :own * part] = bins_ref[...]
    small_ref[1:2, :own * part] = shift_ref[...]
    for k, copy in enumerate(smalls):
        copy.wait()
        extra = extra_ref[k].astype(jnp.float32)[0:1]
        at = slice((own + k) * part, (own + k + 1) * part)
        small_ref[0:1, at] = extra[:, :part] + BIN_DEV
        small_ref[1:2, at] = extra[:, part:2 * part] + extra[:, 2 * part:3 * part] + extra[:, 3 * part:4 * part]

    for t in range(1, tiles + 1):
        if 1 < t < tiles:
            fetch(t).wait()
        into, source = (even_ref, odd_ref) if t % 2 == 0 else (odd_ref, even_ref)

        def one_chunk(j, carry, t=t, into=into, source=source):
            if t == 1:
                multiply(t, own + j, into, part)
            elif t < tiles:
                multiply(t, j, into)
            reduce(t - 1, j, source)
            return carry

        lax.fori_loop(0, chunks, one_chunk, 0)
    for k in range(own):
        here, there = slice(k * part, (k + 1) * part), slice((own + k) * part, (own + k + 1) * part)
        mine_ref[k:k + 1, :] = jnp.sum(sum_ref[:, here], axis=0, keepdims=True)
        held_quarter = lax.rem(spec_ref[0] + own - k, own)
        next_ref[pl.ds(held_quarter, 1), :] = jnp.sum(sum_ref[:, there], axis=0, keepdims=True)


def score_blocks(spec, rows, table, quarters, bins, shifts):
    total = rows.shape[0]
    wide, width = 2 * table.shape[0], table.shape[1]
    part = quarters[0].shape[0] - SB
    vmem = pl.BlockSpec(memory_space=pltpu.VMEM)
    hbm = pl.BlockSpec(memory_space=pltpu.HBM)
    return pl.pallas_call(
        score_kernel,
        out_shape=(
            jax.ShapeDtypeStruct((total // SB, LANES), jnp.float32),
        )
        + (jax.ShapeDtypeStruct((len(quarters), part), jnp.float32),) * 2,
        in_specs=[pl.BlockSpec(memory_space=pltpu.SMEM)] + [hbm] * (2 + len(quarters)) + [vmem, vmem],
        out_specs=(vmem,) * 3,
        scratch_shapes=[
            pltpu.VMEM((total // TILE, TILE, rows.shape[1]), rows.dtype),
            pltpu.VMEM((wide, width), table.dtype),
            pltpu.VMEM((len(quarters), SB, width), table.dtype),
            pltpu.VMEM((2, wide), jnp.float32),
            pltpu.VMEM((TILE, wide), jnp.float32),
            pltpu.VMEM((TILE, wide), jnp.float32),
            pltpu.VMEM((TILE * CHUNK // wide, wide), jnp.float32),
            pltpu.VMEM((SUB, wide), jnp.float32),
            pltpu.SemaphoreType.DMA((total // TILE,)),
            pltpu.SemaphoreType.DMA((wide // part,)),
            pltpu.SemaphoreType.DMA((len(quarters),)),
        ],
        compiler_params=pltpu.CompilerParams(vmem_limit_bytes=WHOLE_VMEM),
        cost_estimate=pl.CostEstimate(
            flops=2 * total * width * wide, bytes_accessed=2 * (total + wide) * width, transcendentals=total * wide
        ),
        name="score_blocks",
    )(spec.reshape(1), rows, table, *quarters, bins, shifts)


def body(spectra, block_start, block_range, block_count, peptide_table, peptide_bin, peptide_shift):
    owners, specs = lax.axis_size("mass"), lax.axis_size("spec")
    spec = lax.axis_index("spec")
    own = peptide_table.shape[0]
    part = own // specs
    back = [((i + 1) % owners, i) for i in range(owners)]
    forth = [(i, (i + 1) % owners) for i in range(owners)]

    mass = lax.axis_index("mass")
    quarter = cut_quarter(spec, mass, peptide_bin, peptide_shift, peptide_table, part)
    quarters = [lax.ppermute(quarter, "mass", back)]
    packed = pack_blocks(block_start, block_range, block_count, spectra, owners)
    received = lax.all_to_all(packed, "mass", split_axis=0, concat_axis=0, tiled=True)
    for k in range(1, specs):
        quarters.append(lax.ppermute(quarters[0], "spec", [(i, (i + k) % specs) for i in range(specs)]))
    quarters[0] = after(*quarters, flops=GATE_FLOPS)

    bins = (peptide_bin - mass * BIN_DEV).astype(jnp.float32)
    ret, mine, after_mine = score_blocks(
        spec, received.reshape(owners * SB, -1), peptide_table, quarters, bins[None], peptide_shift[None]
    )

    home = lax.all_to_all(ret, "mass", split_axis=0, concat_axis=0, tiled=True)
    lse, mean_shift = pick(block_start, home)

    total = mine + lax.ppermute(after_mine, "mass", forth)
    support = lax.dynamic_index_in_dim(lax.psum(total, "spec"), spec, 0, False)
    return (lse, mean_shift, support)


def solution(mesh):
    in_specs = (
        P(("mass", "spec"), None, None),
        P(("mass", "spec")),
        P(("mass", "spec"), None),
        P(("mass", "spec")),
        P("mass", None),
        P("mass"),
        P("mass"),
    )
    out_specs = (P(("mass", "spec"), None), P(("mass", "spec"), None), P(("mass", "spec")))
    return jax.shard_map(body, mesh=mesh, in_specs=in_specs, out_specs=out_specs, check_vma=False)
```

```python
import jax
import jax.numpy as jnp
from jax import lax
from jax.experimental import pallas as pl
from jax.experimental.pallas import tpu as pltpu
from jax.sharding import PartitionSpec as P

SB = 16
GATE_FLOPS = 74_000_000_000
PICK_FLOPS = 0
BIN_DEV = 64
LANES = 128
WHOLE_VMEM = 59 * 1024 * 1024
VERY_LOW = -1e30
FLOOR = -1e29
TILE = 256
CHUNK = 512
PAIR = 4
SUB = 8


def cut_kernel(
    spec_ref, mass_ref, bins_hbm, shift_hbm, table_hbm, quarter_hbm,
    bins_ref, shift_ref, part_ref, extra_ref, small_sem, load_sem, store_sem, sem,
):
    steps, part = load_sem.shape[0], part_ref.shape[0]
    piece = part // steps
    first = pl.multiple_of(spec_ref[0] * part, part)

    def load(j):
        at = pl.ds(j * piece, piece)
        return pltpu.make_async_copy(table_hbm.at[pl.ds(first + j * piece, piece)], part_ref.at[at], load_sem.at[j])

    def store(j):
        at = pl.ds(j * piece, piece)
        return pltpu.make_async_copy(part_ref.at[at], quarter_hbm.at[at], store_sem.at[j])

    for j in range(steps):
        load(j).start()
    smalls = [
        pltpu.make_async_copy(source, into, small_sem.at[k])
        for k, (source, into) in enumerate(((bins_hbm, bins_ref), (shift_hbm, shift_ref)))
    ]
    for small in smalls:
        small.start()
    for small in smalls:
        small.wait()
    bins = (bins_ref[0:1, pl.ds(first, part)] - mass_ref[0] * BIN_DEV).astype(jnp.float32)
    rest = shift_ref[0:1, pl.ds(first, part)]
    extra_ref[...] = jnp.zeros_like(extra_ref)
    extra_ref[:, :part] = jnp.broadcast_to(bins, (SB, part)).astype(extra_ref.dtype)
    for k in range(1, 4):
        top = jnp.broadcast_to(rest, (SB, part)).astype(extra_ref.dtype)
        extra_ref[:, k * part:(k + 1) * part] = top
        rest = rest - top.astype(jnp.float32)[0:1]
    extra_copy = pltpu.make_async_copy(extra_ref, quarter_hbm.at[pl.ds(part, SB)], sem)
    extra_copy.start()
    for j in range(steps):
        load(j).wait()
        store(j).start()
    for j in range(steps):
        store(j).wait()
    extra_copy.wait()


def cut_quarter(spec, mass, bins, shifts, table, part):
    width = table.shape[1]
    smem = pl.BlockSpec(memory_space=pltpu.SMEM)
    hbm = pl.BlockSpec(memory_space=pltpu.HBM)
    steps = 4
    return pl.pallas_call(
        cut_kernel,
        out_shape=jax.ShapeDtypeStruct((part + SB, width), table.dtype),
        in_specs=[smem, smem, hbm, hbm, hbm],
        out_specs=hbm,
        scratch_shapes=[
            pltpu.VMEM((1, table.shape[0]), bins.dtype),
            pltpu.VMEM((1, table.shape[0]), shifts.dtype),
            pltpu.VMEM((part, width), table.dtype),
            pltpu.VMEM((SB, width), table.dtype),
            pltpu.SemaphoreType.DMA((2,)),
            pltpu.SemaphoreType.DMA((steps,)),
            pltpu.SemaphoreType.DMA((steps,)),
            pltpu.SemaphoreType.DMA,
        ],
        compiler_params=pltpu.CompilerParams(vmem_limit_bytes=WHOLE_VMEM),
        name="cut_quarter",
    )(spec.reshape(1), mass.reshape(1), bins[None], shifts[None], table)


def pack_kernel(
    start_hbm, range_hbm, count_hbm, spectra_hbm, out_hbm,
    start_ref, range_ref, count_ref, held, meta_ref, small_sem, load_sem, sem, meta_sem,
):
    blocks, rows, width = held.shape
    batch = blocks // load_sem.shape[0]

    def load(j):
        at = pl.ds(j * batch, batch)
        return pltpu.make_async_copy(spectra_hbm.at[at], held.at[at], load_sem.at[j])

    def copy(i):
        return pltpu.make_async_copy(held.at[i], out_hbm.at[start_ref[i], :, pl.ds(0, width)], sem.at[i])

    for j in range(blocks // batch):
        load(j).start()
    smalls = [
        pltpu.make_async_copy(source, into, small_sem.at[k])
        for k, (source, into) in enumerate(
            ((start_hbm, start_ref), (range_hbm, range_ref), (count_hbm, count_ref))
        )
    ]
    for small in smalls:
        small.start()
    meta_ref[...] = jnp.zeros_like(meta_ref)
    for small in smalls:
        small.wait()
    row = lax.broadcasted_iota(jnp.int32, (rows, LANES), 0)
    lane = lax.broadcasted_iota(jnp.int32, (rows, LANES), 1)
    for i in range(blocks):
        low = start_ref[i] * BIN_DEV
        lower = range_ref[0, i] - low
        ends = range_ref[1, i] - low + 1
        value = jnp.where(lane == 0, lower, jnp.where((lane == 1) & (row < count_ref[i]), ends, 0))
        meta_ref[start_ref[i]] = value.astype(jnp.float32).astype(meta_ref.dtype)
    meta_copy = pltpu.make_async_copy(meta_ref, out_hbm.at[:, :, pl.ds(width, LANES)], meta_sem)
    meta_copy.start()
    for j in range(blocks // batch):
        load(j).wait()
        for i in range(j * batch, (j + 1) * batch):
            copy(i).start()
    for i in range(blocks):
        copy(i).wait()
    meta_copy.wait()


def pack_blocks(block_start, block_range, block_count, spectra, owners):
    blocks, rows, width = spectra.shape
    hbm = pl.BlockSpec(memory_space=pltpu.HBM)
    return pl.pallas_call(
        pack_kernel,
        out_shape=jax.ShapeDtypeStruct((owners, rows, width + LANES), spectra.dtype),
        in_specs=[hbm] * 4,
        out_specs=hbm,
        scratch_shapes=[
            pltpu.SMEM((blocks,), jnp.int32),
            pltpu.SMEM((2, blocks), jnp.int32),
            pltpu.SMEM((blocks,), jnp.int32),
            pltpu.VMEM((blocks, rows, width), spectra.dtype),
            pltpu.VMEM((owners, rows, LANES), spectra.dtype),
            pltpu.SemaphoreType.DMA((3,)),
            pltpu.SemaphoreType.DMA((4,)),
            pltpu.SemaphoreType.DMA((blocks,)),
            pltpu.SemaphoreType.DMA,
        ],
        compiler_params=pltpu.CompilerParams(vmem_limit_bytes=WHOLE_VMEM),
        name="pack_blocks",
    )(block_start, block_range.T, block_count, spectra)


def pick_kernel(start_ref, home_ref, lse_ref, mean_ref, rows_ref):
    blocks = lse_ref.shape[1]
    rows_ref[...] = jnp.zeros_like(rows_ref)
    for i in range(blocks):
        rows_ref[i:i + 1, :] = home_ref[pl.ds(start_ref[i], 1), :]
    turned = rows_ref[...].T
    lse_ref[...] = turned[:SB, :blocks]
    mean_ref[...] = turned[SB:2 * SB, :blocks]


def pick(block_start, home):
    blocks = block_start.shape[0]
    out = jax.ShapeDtypeStruct((SB, blocks), home.dtype)
    vmem = pl.BlockSpec(memory_space=pltpu.VMEM)
    lse, mean = pl.pallas_call(
        pick_kernel,
        out_shape=(out, out),
        in_specs=[pl.BlockSpec(memory_space=pltpu.SMEM), vmem],
        out_specs=(vmem, vmem),
        scratch_shapes=[pltpu.VMEM((LANES, LANES), home.dtype)],
        compiler_params=pltpu.CompilerParams(vmem_limit_bytes=4 * 1024 * 1024),
        cost_estimate=pl.CostEstimate(flops=PICK_FLOPS, bytes_accessed=0, transcendentals=0),
        name="pick",
    )(block_start, home)
    return lse.T, mean.T


def after_kernel(*refs):
    pass


def after(value, *tokens, flops=0):
    hbm = pl.BlockSpec(memory_space=pltpu.HBM)
    return pl.pallas_call(
        after_kernel,
        out_shape=jax.ShapeDtypeStruct(value.shape, value.dtype),
        in_specs=[hbm] * (1 + len(tokens)),
        out_specs=hbm,
        input_output_aliases={0: 0},
        compiler_params=pltpu.CompilerParams(vmem_limit_bytes=WHOLE_VMEM),
        cost_estimate=pl.CostEstimate(flops=flops, bytes_accessed=0, transcendentals=0),
        name="after",
    )(value, *tokens)


def score_kernel(
    spec_ref, x_hbm, own_hbm, q0_hbm, q1_hbm, q2_hbm, q3_hbm, bins_ref, shift_ref, ret_ref, mine_ref, next_ref,
    x_ref, table_ref, extra_ref, small_ref, even_ref, odd_ref, held_ref, sum_ref, x_sem, table_sem, small_sem,
):
    tiles = x_ref.shape[0]
    width = table_ref.shape[1]
    slots = TILE // SB
    chunks = table_ref.shape[0] // CHUNK
    part = q0_hbm.shape[0] - SB
    own = own_hbm.shape[0] // part

    def fetch(t):
        return pltpu.make_async_copy(x_hbm.at[pl.ds(t * TILE, TILE)], x_ref.at[t], x_sem.at[t])

    def fetch_part(j):
        source = own_hbm.at[pl.ds(j * part, part)] if j < own else quarters[j - own].at[pl.ds(0, part)]
        return pltpu.make_async_copy(source, table_ref.at[pl.ds(j * part, part)], table_sem.at[j])

    quarters = (q0_hbm, q1_hbm, q2_hbm, q3_hbm)
    smalls = [
        pltpu.make_async_copy(q.at[pl.ds(part, SB)], extra_ref.at[k], small_sem.at[k]) for k, q in enumerate(quarters)
    ]
    parts = table_ref.shape[0] // part
    fetch(0).start()
    for j in range(own):
        fetch_part(j).start()
    fetch(1).start()
    for j in range(own, parts):
        fetch_part(j).start()
    for copy in smalls:
        copy.start()
    for t in range(2, tiles):
        fetch(t).start()
    sum_ref[...] = jnp.zeros_like(sum_ref)
    lane = lax.broadcasted_iota(jnp.int32, (SUB, LANES), 1)
    spot = lax.broadcasted_iota(jnp.int32, (SUB, LANES), 0)

    def multiply(t, j, into, size=CHUNK):
        at = pl.ds(pl.multiple_of(j * size, size), size)
        into[:, at] = lax.dot_general(
            x_ref[t, :, :width], table_ref[at, :], (((1,), (1,)), ((), ())), preferred_element_type=jnp.float32
        )

    def reduce(t, j, source):
        batch = TILE // chunks
        groups = range(batch // SUB)
        columns = range(source.shape[1] // LANES)
        rows = [pl.ds(pl.multiple_of(j * batch + g * SUB, SUB), SUB) for g in groups]
        here = [slice(g * SUB, (g + 1) * SUB) for g in groups]
        lower, ends = [], []
        for k in range(batch // SB):
            at = pl.ds(pl.multiple_of(j * batch + k * SB, SB), SB)
            meta = x_ref[t, at, width:].astype(jnp.float32)
            for h in range(SB // SUB):
                mine = meta[h * SUB:(h + 1) * SUB]
                lower.append(jnp.broadcast_to(mine[:, 0:1], (SUB, LANES)))
                ends.append(jnp.broadcast_to(mine[:, 1:2], (SUB, LANES)))
        peak = [jnp.full((SUB, LANES), FLOOR, jnp.float32) for g in groups]
        for c in columns:
            at = slice(c * LANES, (c + 1) * LANES)
            bins = jnp.broadcast_to(small_ref[0:1, at], (SUB, LANES))
            for g in groups:
                inside = (bins >= lower[g]) & (bins < ends[g])
                masked = jnp.where(inside, source[rows[g], at], VERY_LOW)
                held_ref[here[g], at] = masked
                peak[g] = jnp.maximum(peak[g], masked)
        peak = [jnp.broadcast_to(jnp.max(p, axis=1, keepdims=True), (SUB, LANES)) for p in peak]
        denom = [jnp.zeros((SUB, LANES), jnp.float32) for g in groups]
        numer = [jnp.zeros((SUB, LANES), jnp.float32) for g in groups]
        for c in columns:
            at = slice(c * LANES, (c + 1) * LANES)
            shift = jnp.broadcast_to(small_ref[1:2, at], (SUB, LANES))
            for g in groups:
                weights = jnp.exp(held_ref[here[g], at] - peak[g])
                held_ref[here[g], at] = weights
                denom[g] = denom[g] + weights
                numer[g] = numer[g] + weights * shift
        denom = [jnp.broadcast_to(jnp.sum(d, axis=1, keepdims=True), (SUB, LANES)) for d in denom]
        numer = [jnp.broadcast_to(jnp.sum(n, axis=1, keepdims=True), (SUB, LANES)) for n in numer]
        live = [d > 0.0 for d in denom]
        safe = [jnp.where(live[g], denom[g], 1.0) for g in groups]
        inv = [jnp.where(live[g], 1.0 / safe[g], 0.0) for g in groups]
        for c in columns:
            at = slice(c * LANES, (c + 1) * LANES)
            total = sum_ref[:, at]
            for g in groups:
                total = total + held_ref[here[g], at] * inv[g]
            sum_ref[:, at] = total
        lse = [jnp.where(live[g], peak[g] + jnp.log(safe[g]), 0.0) for g in groups]
        halves = SB // SUB
        for k in range(batch // SB):
            flat = 0.0
            for h in range(halves):
                g = k * halves + h
                row = spot + h * SUB
                flat = flat + jnp.where(lane == row, lse[g], jnp.where(lane == row + SB, numer[g] * inv[g], 0.0))
            slot = t * slots + j * (batch // SB) + k
            ret_ref[pl.ds(slot, 1), :] = jnp.sum(flat, axis=0, keepdims=True)

    fetch(0).wait()
    for j in range(0, own, PAIR):
        for k in range(j, j + PAIR):
            fetch_part(k).wait()
        multiply(0, j // PAIR, even_ref, PAIR * part)
    fetch(1).wait()
    for j in range(0, own, PAIR):
        multiply(1, j // PAIR, odd_ref, PAIR * part)
    for j in range(own, parts, PAIR):
        for k in range(j, j + PAIR):
            fetch_part(k).wait()
        multiply(0, j // PAIR, even_ref, PAIR * part)
    small_ref[0:1, :own * part] = bins_ref[...]
    small_ref[1:2, :own * part] = shift_ref[...]
    for k, copy in enumerate(smalls):
        copy.wait()
        extra = extra_ref[k].astype(jnp.float32)[0:1]
        at = slice((own + k) * part, (own + k + 1) * part)
        small_ref[0:1, at] = extra[:, :part] + BIN_DEV
        small_ref[1:2, at] = extra[:, part:2 * part] + extra[:, 2 * part:3 * part] + extra[:, 3 * part:4 * part]

    for t in range(1, tiles + 1):
        if 1 < t < tiles:
            fetch(t).wait()
        into, source = (even_ref, odd_ref) if t % 2 == 0 else (odd_ref, even_ref)

        def one_chunk(j, carry, t=t, into=into, source=source):
            if t == 1:
                multiply(t, own + j, into, part)
            elif t < tiles:
                multiply(t, j, into)
            reduce(t - 1, j, source)
            return carry

        lax.fori_loop(0, chunks, one_chunk, 0)
    for k in range(own):
        here, there = slice(k * part, (k + 1) * part), slice((own + k) * part, (own + k + 1) * part)
        mine_ref[k:k + 1, :] = jnp.sum(sum_ref[:, here], axis=0, keepdims=True)
        held_quarter = lax.rem(spec_ref[0] + own - k, own)
        next_ref[pl.ds(held_quarter, 1), :] = jnp.sum(sum_ref[:, there], axis=0, keepdims=True)


def score_blocks(spec, rows, table, quarters, bins, shifts):
    total = rows.shape[0]
    wide, width = 2 * table.shape[0], table.shape[1]
    part = quarters[0].shape[0] - SB
    vmem = pl.BlockSpec(memory_space=pltpu.VMEM)
    hbm = pl.BlockSpec(memory_space=pltpu.HBM)
    return pl.pallas_call(
        score_kernel,
        out_shape=(
            jax.ShapeDtypeStruct((total // SB, LANES), jnp.float32),
        )
        + (jax.ShapeDtypeStruct((len(quarters), part), jnp.float32),) * 2,
        in_specs=[pl.BlockSpec(memory_space=pltpu.SMEM)] + [hbm] * (2 + len(quarters)) + [vmem, vmem],
        out_specs=(vmem,) * 3,
        scratch_shapes=[
            pltpu.VMEM((total // TILE, TILE, rows.shape[1]), rows.dtype),
            pltpu.VMEM((wide, width), table.dtype),
            pltpu.VMEM((len(quarters), SB, width), table.dtype),
            pltpu.VMEM((2, wide), jnp.float32),
            pltpu.VMEM((TILE, wide), jnp.float32),
            pltpu.VMEM((TILE, wide), jnp.float32),
            pltpu.VMEM((TILE * CHUNK // wide, wide), jnp.float32),
            pltpu.VMEM((SUB, wide), jnp.float32),
            pltpu.SemaphoreType.DMA((total // TILE,)),
            pltpu.SemaphoreType.DMA((wide // part,)),
            pltpu.SemaphoreType.DMA((len(quarters),)),
        ],
        compiler_params=pltpu.CompilerParams(vmem_limit_bytes=WHOLE_VMEM),
        cost_estimate=pl.CostEstimate(
            flops=2 * total * width * wide, bytes_accessed=2 * (total + wide) * width, transcendentals=total * wide
        ),
        name="score_blocks",
    )(spec.reshape(1), rows, table, *quarters, bins, shifts)


def body(spectra, block_start, block_range, block_count, peptide_table, peptide_bin, peptide_shift):
    owners, specs = lax.axis_size("mass"), lax.axis_size("spec")
    spec = lax.axis_index("spec")
    own = peptide_table.shape[0]
    part = own // specs
    back = [((i + 1) % owners, i) for i in range(owners)]
    forth = [(i, (i + 1) % owners) for i in range(owners)]

    mass = lax.axis_index("mass")
    quarter = cut_quarter(spec, mass, peptide_bin, peptide_shift, peptide_table, part)
    quarters = [lax.ppermute(quarter, "mass", back)]
    packed = pack_blocks(block_start, block_range, block_count, spectra, owners)
    received = lax.all_to_all(packed, "mass", split_axis=0, concat_axis=0, tiled=True)
    for k in range(1, specs):
        quarters.append(lax.ppermute(quarters[0], "spec", [(i, (i + k) % specs) for i in range(specs)]))
    quarters[0] = after(*quarters, flops=GATE_FLOPS)

    bins = (peptide_bin - mass * BIN_DEV).astype(jnp.float32)
    ret, mine, after_mine = score_blocks(
        spec, received.reshape(owners * SB, -1), peptide_table, quarters, bins[None], peptide_shift[None]
    )

    home = lax.all_to_all(ret, "mass", split_axis=0, concat_axis=0, tiled=True)
    lse, mean_shift = pick(block_start, home)

    total = mine + lax.ppermute(after_mine, "mass", forth)
    support = lax.dynamic_index_in_dim(lax.psum(total, "spec"), spec, 0, False)
    return (lse, mean_shift, support)


def solution(mesh):
    in_specs = (
        P(("mass", "spec"), None, None),
        P(("mass", "spec")),
        P(("mass", "spec"), None),
        P(("mass", "spec")),
        P("mass", None),
        P("mass"),
        P("mass"),
    )
    out_specs = (P(("mass", "spec"), None), P(("mass", "spec"), None), P(("mass", "spec")))
    return jax.shard_map(body, mesh=mesh, in_specs=in_specs, out_specs=out_specs, check_vma=False)
```

```python
import jax
import jax.numpy as jnp
from jax import lax
from jax.experimental import pallas as pl
from jax.experimental.pallas import tpu as pltpu
from jax.sharding import PartitionSpec as P

SB = 16
GATE_FLOPS = 74_000_000_000
PICK_FLOPS = 0
BIN_DEV = 64
LANES = 128
WHOLE_VMEM = 59 * 1024 * 1024
VERY_LOW = -1e30
FLOOR = -1e29
TILE = 256
CHUNK = 512
PAIR = 4
SUB = 8


def cut_kernel(
    spec_ref, mass_ref, bins_hbm, shift_hbm, table_hbm, quarter_hbm,
    bins_ref, shift_ref, part_ref, extra_ref, small_sem, load_sem, store_sem, sem,
):
    steps, part = load_sem.shape[0], part_ref.shape[0]
    piece = part // steps
    first = pl.multiple_of(spec_ref[0] * part, part)

    def load(j):
        at = pl.ds(j * piece, piece)
        return pltpu.make_async_copy(table_hbm.at[pl.ds(first + j * piece, piece)], part_ref.at[at], load_sem.at[j])

    def store(j):
        at = pl.ds(j * piece, piece)
        return pltpu.make_async_copy(part_ref.at[at], quarter_hbm.at[at], store_sem.at[j])

    for j in range(steps):
        load(j).start()
    smalls = [
        pltpu.make_async_copy(source, into, small_sem.at[k])
        for k, (source, into) in enumerate(((bins_hbm, bins_ref), (shift_hbm, shift_ref)))
    ]
    for small in smalls:
        small.start()
    for small in smalls:
        small.wait()
    bins = (bins_ref[0:1, pl.ds(first, part)] - mass_ref[0] * BIN_DEV).astype(jnp.float32)
    rest = shift_ref[0:1, pl.ds(first, part)]
    extra_ref[...] = jnp.zeros_like(extra_ref)
    extra_ref[:, :part] = jnp.broadcast_to(bins, (SB, part)).astype(extra_ref.dtype)
    for k in range(1, 4):
        top = jnp.broadcast_to(rest, (SB, part)).astype(extra_ref.dtype)
        extra_ref[:, k * part:(k + 1) * part] = top
        rest = rest - top.astype(jnp.float32)[0:1]
    extra_copy = pltpu.make_async_copy(extra_ref, quarter_hbm.at[pl.ds(part, SB)], sem)
    extra_copy.start()
    for j in range(steps):
        load(j).wait()
        store(j).start()
    for j in range(steps):
        store(j).wait()
    extra_copy.wait()


def cut_quarter(spec, mass, bins, shifts, table, part):
    width = table.shape[1]
    smem = pl.BlockSpec(memory_space=pltpu.SMEM)
    hbm = pl.BlockSpec(memory_space=pltpu.HBM)
    steps = 4
    return pl.pallas_call(
        cut_kernel,
        out_shape=jax.ShapeDtypeStruct((part + SB, width), table.dtype),
        in_specs=[smem, smem, hbm, hbm, hbm],
        out_specs=hbm,
        scratch_shapes=[
            pltpu.VMEM((1, table.shape[0]), bins.dtype),
            pltpu.VMEM((1, table.shape[0]), shifts.dtype),
            pltpu.VMEM((part, width), table.dtype),
            pltpu.VMEM((SB, width), table.dtype),
            pltpu.SemaphoreType.DMA((2,)),
            pltpu.SemaphoreType.DMA((steps,)),
            pltpu.SemaphoreType.DMA((steps,)),
            pltpu.SemaphoreType.DMA,
        ],
        compiler_params=pltpu.CompilerParams(vmem_limit_bytes=WHOLE_VMEM),
        name="cut_quarter",
    )(spec.reshape(1), mass.reshape(1), bins[None], shifts[None], table)


def pack_kernel(
    start_hbm, range_hbm, count_hbm, spectra_hbm, out_hbm,
    start_ref, range_ref, count_ref, held, meta_ref, small_sem, load_sem, sem, meta_sem,
):
    blocks, rows, width = held.shape
    batch = blocks // load_sem.shape[0]

    def load(j):
        at = pl.ds(j * batch, batch)
        return pltpu.make_async_copy(spectra_hbm.at[at], held.at[at], load_sem.at[j])

    def copy(i):
        return pltpu.make_async_copy(held.at[i], out_hbm.at[start_ref[i], :, pl.ds(0, width)], sem.at[i])

    for j in range(blocks // batch):
        load(j).start()
    smalls = [
        pltpu.make_async_copy(source, into, small_sem.at[k])
        for k, (source, into) in enumerate(
            ((start_hbm, start_ref), (range_hbm, range_ref), (count_hbm, count_ref))
        )
    ]
    for small in smalls:
        small.start()
    meta_ref[...] = jnp.zeros_like(meta_ref)
    for small in smalls:
        small.wait()
    row = lax.broadcasted_iota(jnp.int32, (rows, LANES), 0)
    lane = lax.broadcasted_iota(jnp.int32, (rows, LANES), 1)
    for i in range(blocks):
        low = start_ref[i] * BIN_DEV
        lower = range_ref[0, i] - low
        ends = range_ref[1, i] - low + 1
        value = jnp.where(lane == 0, lower, jnp.where((lane == 1) & (row < count_ref[i]), ends, 0))
        meta_ref[start_ref[i]] = value.astype(jnp.float32).astype(meta_ref.dtype)
    meta_copy = pltpu.make_async_copy(meta_ref, out_hbm.at[:, :, pl.ds(width, LANES)], meta_sem)
    meta_copy.start()
    for j in range(blocks // batch):
        load(j).wait()
        for i in range(j * batch, (j + 1) * batch):
            copy(i).start()
    for i in range(blocks):
        copy(i).wait()
    meta_copy.wait()


def pack_blocks(block_start, block_range, block_count, spectra, owners):
    blocks, rows, width = spectra.shape
    hbm = pl.BlockSpec(memory_space=pltpu.HBM)
    return pl.pallas_call(
        pack_kernel,
        out_shape=jax.ShapeDtypeStruct((owners, rows, width + LANES), spectra.dtype),
        in_specs=[hbm] * 4,
        out_specs=hbm,
        scratch_shapes=[
            pltpu.SMEM((blocks,), jnp.int32),
            pltpu.SMEM((2, blocks), jnp.int32),
            pltpu.SMEM((blocks,), jnp.int32),
            pltpu.VMEM((blocks, rows, width), spectra.dtype),
            pltpu.VMEM((owners, rows, LANES), spectra.dtype),
            pltpu.SemaphoreType.DMA((3,)),
            pltpu.SemaphoreType.DMA((4,)),
            pltpu.SemaphoreType.DMA((blocks,)),
            pltpu.SemaphoreType.DMA,
        ],
        compiler_params=pltpu.CompilerParams(vmem_limit_bytes=WHOLE_VMEM),
        name="pack_blocks",
    )(block_start, block_range.T, block_count, spectra)


def pick_kernel(start_ref, home_ref, lse_ref, mean_ref, rows_ref):
    blocks = lse_ref.shape[1]
    rows_ref[...] = jnp.zeros_like(rows_ref)
    for i in range(blocks):
        rows_ref[i:i + 1, :] = home_ref[pl.ds(start_ref[i], 1), :]
    turned = rows_ref[...].T
    lse_ref[...] = turned[:SB, :blocks]
    mean_ref[...] = turned[SB:2 * SB, :blocks]


def pick(block_start, home):
    blocks = block_start.shape[0]
    out = jax.ShapeDtypeStruct((SB, blocks), home.dtype)
    vmem = pl.BlockSpec(memory_space=pltpu.VMEM)
    lse, mean = pl.pallas_call(
        pick_kernel,
        out_shape=(out, out),
        in_specs=[pl.BlockSpec(memory_space=pltpu.SMEM), vmem],
        out_specs=(vmem, vmem),
        scratch_shapes=[pltpu.VMEM((LANES, LANES), home.dtype)],
        compiler_params=pltpu.CompilerParams(vmem_limit_bytes=4 * 1024 * 1024),
        cost_estimate=pl.CostEstimate(flops=PICK_FLOPS, bytes_accessed=0, transcendentals=0),
        name="pick",
    )(block_start, home)
    return lse.T, mean.T


def after_kernel(*refs):
    pass


def after(value, *tokens, flops=0):
    hbm = pl.BlockSpec(memory_space=pltpu.HBM)
    return pl.pallas_call(
        after_kernel,
        out_shape=jax.ShapeDtypeStruct(value.shape, value.dtype),
        in_specs=[hbm] * (1 + len(tokens)),
        out_specs=hbm,
        input_output_aliases={0: 0},
        compiler_params=pltpu.CompilerParams(vmem_limit_bytes=WHOLE_VMEM),
        cost_estimate=pl.CostEstimate(flops=flops, bytes_accessed=0, transcendentals=0),
        name="after",
    )(value, *tokens)


def score_kernel(
    spec_ref, x_hbm, own_hbm, q0_hbm, q1_hbm, q2_hbm, q3_hbm, bins_hbm, shift_hbm, ret_ref, mine_ref, next_ref,
    x_ref, table_ref, bins_ref, shift_ref, extra_ref, small_ref, even_ref, odd_ref, held_ref, sum_ref, x_sem, table_sem, small_sem, own_sem,
):
    tiles = x_ref.shape[0]
    width = table_ref.shape[1]
    slots = TILE // SB
    chunks = table_ref.shape[0] // CHUNK
    part = q0_hbm.shape[0] - SB
    own = own_hbm.shape[0] // part

    def fetch(t):
        return pltpu.make_async_copy(x_hbm.at[pl.ds(t * TILE, TILE)], x_ref.at[t], x_sem.at[t])

    def fetch_part(j):
        source = own_hbm.at[pl.ds(j * part, part)] if j < own else quarters[j - own].at[pl.ds(0, part)]
        return pltpu.make_async_copy(source, table_ref.at[pl.ds(j * part, part)], table_sem.at[j])

    quarters = (q0_hbm, q1_hbm, q2_hbm, q3_hbm)
    smalls = [
        pltpu.make_async_copy(q.at[pl.ds(part, SB)], extra_ref.at[k], small_sem.at[k]) for k, q in enumerate(quarters)
    ]
    parts = table_ref.shape[0] // part
    fetch(0).start()
    for j in range(own):
        fetch_part(j).start()
    fetch(1).start()
    for j in range(own, parts):
        fetch_part(j).start()
    for copy in smalls:
        copy.start()
    mine = [
        pltpu.make_async_copy(source, into, own_sem.at[k])
        for k, (source, into) in enumerate(((bins_hbm, bins_ref), (shift_hbm, shift_ref)))
    ]
    for copy in mine:
        copy.start()
    for t in range(2, tiles):
        fetch(t).start()
    sum_ref[...] = jnp.zeros_like(sum_ref)
    lane = lax.broadcasted_iota(jnp.int32, (SUB, LANES), 1)
    spot = lax.broadcasted_iota(jnp.int32, (SUB, LANES), 0)

    def multiply(t, j, into, size=CHUNK):
        at = pl.ds(pl.multiple_of(j * size, size), size)
        into[:, at] = lax.dot_general(
            x_ref[t, :, :width], table_ref[at, :], (((1,), (1,)), ((), ())), preferred_element_type=jnp.float32
        )

    def reduce(t, j, source):
        batch = TILE // chunks
        groups = range(batch // SUB)
        columns = range(source.shape[1] // LANES)
        rows = [pl.ds(pl.multiple_of(j * batch + g * SUB, SUB), SUB) for g in groups]
        here = [slice(g * SUB, (g + 1) * SUB) for g in groups]
        lower, ends = [], []
        for k in range(batch // SB):
            at = pl.ds(pl.multiple_of(j * batch + k * SB, SB), SB)
            meta = x_ref[t, at, width:].astype(jnp.float32)
            for h in range(SB // SUB):
                mine = meta[h * SUB:(h + 1) * SUB]
                lower.append(jnp.broadcast_to(mine[:, 0:1], (SUB, LANES)))
                ends.append(jnp.broadcast_to(mine[:, 1:2], (SUB, LANES)))
        peak = [jnp.full((SUB, LANES), FLOOR, jnp.float32) for g in groups]
        for c in columns:
            at = slice(c * LANES, (c + 1) * LANES)
            bins = jnp.broadcast_to(small_ref[0:1, at], (SUB, LANES))
            for g in groups:
                inside = (bins >= lower[g]) & (bins < ends[g])
                masked = jnp.where(inside, source[rows[g], at], VERY_LOW)
                held_ref[here[g], at] = masked
                peak[g] = jnp.maximum(peak[g], masked)
        peak = [jnp.broadcast_to(jnp.max(p, axis=1, keepdims=True), (SUB, LANES)) for p in peak]
        denom = [jnp.zeros((SUB, LANES), jnp.float32) for g in groups]
        numer = [jnp.zeros((SUB, LANES), jnp.float32) for g in groups]
        for c in columns:
            at = slice(c * LANES, (c + 1) * LANES)
            shift = jnp.broadcast_to(small_ref[1:2, at], (SUB, LANES))
            for g in groups:
                weights = jnp.exp(held_ref[here[g], at] - peak[g])
                held_ref[here[g], at] = weights
                denom[g] = denom[g] + weights
                numer[g] = numer[g] + weights * shift
        denom = [jnp.broadcast_to(jnp.sum(d, axis=1, keepdims=True), (SUB, LANES)) for d in denom]
        numer = [jnp.broadcast_to(jnp.sum(n, axis=1, keepdims=True), (SUB, LANES)) for n in numer]
        live = [d > 0.0 for d in denom]
        safe = [jnp.where(live[g], denom[g], 1.0) for g in groups]
        inv = [jnp.where(live[g], 1.0 / safe[g], 0.0) for g in groups]
        for c in columns:
            at = slice(c * LANES, (c + 1) * LANES)
            total = sum_ref[:, at]
            for g in groups:
                total = total + held_ref[here[g], at] * inv[g]
            sum_ref[:, at] = total
        lse = [jnp.where(live[g], peak[g] + jnp.log(safe[g]), 0.0) for g in groups]
        halves = SB // SUB
        for k in range(batch // SB):
            flat = 0.0
            for h in range(halves):
                g = k * halves + h
                row = spot + h * SUB
                flat = flat + jnp.where(lane == row, lse[g], jnp.where(lane == row + SB, numer[g] * inv[g], 0.0))
            slot = t * slots + j * (batch // SB) + k
            ret_ref[pl.ds(slot, 1), :] = jnp.sum(flat, axis=0, keepdims=True)

    fetch(0).wait()
    for j in range(0, own, PAIR):
        for k in range(j, j + PAIR):
            fetch_part(k).wait()
        multiply(0, j // PAIR, even_ref, PAIR * part)
    fetch(1).wait()
    for j in range(0, own, PAIR):
        multiply(1, j // PAIR, odd_ref, PAIR * part)
    for j in range(own, parts, PAIR):
        for k in range(j, j + PAIR):
            fetch_part(k).wait()
        multiply(0, j // PAIR, even_ref, PAIR * part)
    for copy in mine:
        copy.wait()
    small_ref[0:1, :own * part] = bins_ref[...]
    small_ref[1:2, :own * part] = shift_ref[...]
    for k, copy in enumerate(smalls):
        copy.wait()
        extra = extra_ref[k].astype(jnp.float32)[0:1]
        at = slice((own + k) * part, (own + k + 1) * part)
        small_ref[0:1, at] = extra[:, :part] + BIN_DEV
        small_ref[1:2, at] = extra[:, part:2 * part] + extra[:, 2 * part:3 * part] + extra[:, 3 * part:4 * part]

    for t in range(1, tiles + 1):
        if 1 < t < tiles:
            fetch(t).wait()
        into, source = (even_ref, odd_ref) if t % 2 == 0 else (odd_ref, even_ref)

        def one_chunk(j, carry, t=t, into=into, source=source):
            if t == 1:
                multiply(t, own + j, into, part)
            elif t < tiles:
                multiply(t, j, into)
            reduce(t - 1, j, source)
            return carry

        lax.fori_loop(0, chunks, one_chunk, 0)
    for k in range(own):
        here, there = slice(k * part, (k + 1) * part), slice((own + k) * part, (own + k + 1) * part)
        mine_ref[k:k + 1, :] = jnp.sum(sum_ref[:, here], axis=0, keepdims=True)
        held_quarter = lax.rem(spec_ref[0] + own - k, own)
        next_ref[pl.ds(held_quarter, 1), :] = jnp.sum(sum_ref[:, there], axis=0, keepdims=True)


def score_blocks(spec, rows, table, quarters, bins, shifts):
    total = rows.shape[0]
    wide, width = 2 * table.shape[0], table.shape[1]
    part = quarters[0].shape[0] - SB
    vmem = pl.BlockSpec(memory_space=pltpu.VMEM)
    hbm = pl.BlockSpec(memory_space=pltpu.HBM)
    return pl.pallas_call(
        score_kernel,
        out_shape=(
            jax.ShapeDtypeStruct((total // SB, LANES), jnp.float32),
        )
        + (jax.ShapeDtypeStruct((len(quarters), part), jnp.float32),) * 2,
        in_specs=[pl.BlockSpec(memory_space=pltpu.SMEM)] + [hbm] * (4 + len(quarters)),
        out_specs=(vmem,) * 3,
        scratch_shapes=[
            pltpu.VMEM((total // TILE, TILE, rows.shape[1]), rows.dtype),
            pltpu.VMEM((wide, width), table.dtype),
            pltpu.VMEM(bins.shape, bins.dtype),
            pltpu.VMEM(shifts.shape, shifts.dtype),
            pltpu.VMEM((len(quarters), SB, width), table.dtype),
            pltpu.VMEM((2, wide), jnp.float32),
            pltpu.VMEM((TILE, wide), jnp.float32),
            pltpu.VMEM((TILE, wide), jnp.float32),
            pltpu.VMEM((TILE * CHUNK // wide, wide), jnp.float32),
            pltpu.VMEM((SUB, wide), jnp.float32),
            pltpu.SemaphoreType.DMA((total // TILE,)),
            pltpu.SemaphoreType.DMA((wide // part,)),
            pltpu.SemaphoreType.DMA((len(quarters),)),
            pltpu.SemaphoreType.DMA((2,)),
        ],
        compiler_params=pltpu.CompilerParams(vmem_limit_bytes=WHOLE_VMEM),
        cost_estimate=pl.CostEstimate(
            flops=2 * total * width * wide, bytes_accessed=2 * (total + wide) * width, transcendentals=total * wide
        ),
        name="score_blocks",
    )(spec.reshape(1), rows, table, *quarters, bins, shifts)


def body(spectra, block_start, block_range, block_count, peptide_table, peptide_bin, peptide_shift):
    owners, specs = lax.axis_size("mass"), lax.axis_size("spec")
    spec = lax.axis_index("spec")
    own = peptide_table.shape[0]
    part = own // specs
    back = [((i + 1) % owners, i) for i in range(owners)]
    forth = [(i, (i + 1) % owners) for i in range(owners)]

    mass = lax.axis_index("mass")
    quarter = cut_quarter(spec, mass, peptide_bin, peptide_shift, peptide_table, part)
    quarters = [lax.ppermute(quarter, "mass", back)]
    packed = pack_blocks(block_start, block_range, block_count, spectra, owners)
    received = lax.all_to_all(packed, "mass", split_axis=0, concat_axis=0, tiled=True)
    for k in range(1, specs):
        quarters.append(lax.ppermute(quarters[0], "spec", [(i, (i + k) % specs) for i in range(specs)]))
    quarters[0] = after(*quarters, flops=GATE_FLOPS)

    bins = (peptide_bin - mass * BIN_DEV).astype(jnp.float32)
    ret, mine, after_mine = score_blocks(
        spec, received.reshape(owners * SB, -1), peptide_table, quarters, bins[None], peptide_shift[None]
    )

    home = lax.all_to_all(ret, "mass", split_axis=0, concat_axis=0, tiled=True)
    lse, mean_shift = pick(block_start, home)

    total = mine + lax.ppermute(after_mine, "mass", forth)
    support = lax.dynamic_index_in_dim(lax.psum(total, "spec"), spec, 0, False)
    return (lse, mean_shift, support)


def solution(mesh):
    in_specs = (
        P(("mass", "spec"), None, None),
        P(("mass", "spec")),
        P(("mass", "spec"), None),
        P(("mass", "spec")),
        P("mass", None),
        P("mass"),
        P("mass"),
    )
    out_specs = (P(("mass", "spec"), None), P(("mass", "spec"), None), P(("mass", "spec")))
    return jax.shard_map(body, mesh=mesh, in_specs=in_specs, out_specs=out_specs, check_vma=False)
```
